32 devices in a mesh: dp: 8 (over y, x, core), seq: 4 (over z).
Axes of the slice: x: 2, y: 2, z: 4, core: 2. Of those that a mesh axis runs over, the one named last changes fastest.
Arguments:
- inputs: bfloat16 [16, 2048, 512], P('dp', 'seq'), may hold values from -6 to 6
- segment_ids: int32 [16, 2048], P('dp'), may hold values from 0 to 6, as said below
- cotangent: bfloat16 [16, 2048, 512], P('dp', 'seq'), may hold values from -6 to 6
- norm_attn: float32 [512], replicated, may hold values from 0.1 to 1.9
- norm_mlp: float32 [512], replicated, may hold values from 0.1 to 1.9
- w_query: bfloat16 [512, 512], replicated, may hold values from -0.25 to 0.25
- w_key: bfloat16 [512, 512], replicated, may hold values from -0.25 to 0.25
- w_value: bfloat16 [512, 512], replicated, may hold values from -0.25 to 0.25
- w_out: bfloat16 [512, 512], replicated, may hold values from -1.5 to 1.5
- w_gate: bfloat16 [512, 1376], replicated, may hold values from -0.25 to 0.25
- w_up: bfloat16 [512, 1376], replicated, may hold values from -0.25 to 0.25
- w_down: bfloat16 [1376, 512], replicated, may hold values from -0.15625 to 0.15625
Outputs:
- output: bfloat16 [16, 2048, 512], P('dp', 'seq')
- grad_input: float32 [16, 2048, 512], P('dp', 'seq')
- grad_norm_attn: float32 [512], replicated
- grad_norm_mlp: float32 [512], replicated
- grad_query: float32 [512, 512], replicated
- grad_key: float32 [512, 512], replicated
- grad_value: float32 [512, 512], replicated
- grad_out: float32 [512, 512], replicated
- grad_gate: float32 [512, 1376], replicated
- grad_up: float32 [512, 1376], replicated
- grad_down: float32 [1376, 512], replicated
The draws below stay inside these ranges and needn't reach their ends.
Inputs may be any that keep to these rules, and one draw needn't show every extreme that they name: `segment_ids`: segment ids never fall along a sequence; in every sequence the documents before the middle one end within its first 128 tokens, and the ones after it begin within its last 128 tokens; the first token has id 0 and the last id 6.
All inputs are finite; a program needn't handle non-finite values.
Results may differ from the reference program's by a relative error of at most 0.014.
Values may be sent and summed in bfloat16 or wider, within the bound.
A program may use at most 128 MiB of HBM per device.

```python
import jax
import jax.numpy as jnp
from jax import lax

D = 512
H = 8
FF = 1376
SEQ_LEN = 2048
DOCS = 7
HD = 64
SEQS = 16


def draw_segment_ids(key, part):
    key = jax.random.fold_in(key, 7)
    head_key, tail_key = jax.random.split(key)
    edge_rows = SEQ_LEN // 16
    head_cuts = (DOCS - 1) // 2
    tail_cuts = DOCS - 1 - head_cuts
    early_cuts = jax.random.randint(head_key, (SEQS, head_cuts), 1, edge_rows)
    late_cuts = jax.random.randint(tail_key, (SEQS, tail_cuts), SEQ_LEN - edge_rows + 1, SEQ_LEN)
    boundaries = jnp.concatenate([early_cuts, late_cuts], axis=1)
    positions = jnp.arange(SEQ_LEN, dtype=jnp.int32)
    passed = (boundaries[:, None, :] <= positions[None, :, None]).astype(jnp.int32)
    return jnp.sum(passed, axis=-1).astype(jnp.int32)


def shard_levels(key, extent, shards, smallest, top_value):
    factor_of, own = 1.0, jax.random.fold_in(key, 6)
    for axis_at, blocks in shards:
        heights = jnp.exp(jax.random.uniform(jax.random.fold_in(own, axis_at), (blocks,), jnp.float32, smallest / len(shards), top_value / len(shards)))
        factor_of = factor_of * jnp.repeat(heights, extent[axis_at] // blocks).reshape([-1 if axis == axis_at else 1 for axis in range(len(extent))])
    return factor_of


def bell_draw(own_key, extent, width, bound, pieces=(), held_as=jnp.bfloat16):
    factor_of = shard_levels(own_key, extent, pieces, -0.22, 0.18) if pieces else 1.0
    drawn = jax.random.normal(own_key, extent, jnp.float32) * width * factor_of
    return jnp.minimum(jnp.maximum(drawn, -bound), bound).astype(held_as)


def setup_inputs(seed: int = 0) -> dict:
    splits = jax.random.split(jax.random.key(seed), 13)
    return {
        "inputs": bell_draw(splits[0], (SEQS, SEQ_LEN, D), 1.0, 6.0, ((0, 8), (1, 4))),
        "segment_ids": draw_segment_ids(jax.random.fold_in(splits[12], 71), 0),
        "cotangent": bell_draw(splits[2], (SEQS, SEQ_LEN, D), 1.0, 6.0, ((0, 8), (1, 4))),
        "norm_attn": jnp.clip(1.0 + 0.18 * jax.random.normal(splits[3], (D,), jnp.float32), 0.1, 1.9),
        "norm_mlp": jnp.clip(1.0 + 0.18 * jax.random.normal(splits[4], (D,), jnp.float32), 0.1, 1.9),
        "w_query": bell_draw(splits[5], (D, D), D ** -0.5, 0.25),
        "w_key": bell_draw(splits[6], (D, D), D ** -0.5, 0.25),
        "w_value": bell_draw(splits[7], (D, D), D ** -0.5, 0.25),
        "w_out": bell_draw(splits[8], (D, D), (D // 32) ** -0.5, 1.5),
        "w_gate": bell_draw(splits[9], (D, FF), D ** -0.5, 0.25),
        "w_up": bell_draw(splits[10], (D, FF), D ** -0.5, 0.25),
        "w_down": bell_draw(splits[11], (FF, D), FF ** -0.5, 0.15625),
    }


@jax.custom_vjp
def low(v):
    return lax.optimization_barrier(v.astype(jnp.bfloat16)).astype(jnp.float32)

@jax.custom_vjp
def low_back(v):
    return v

def low_keep(v):
    return (low(v), None)

def low_pass(kept, grad):
    return (grad,)

def back_keep(v):
    return (v, None)

def back_low(kept, grad):
    return (low(grad),)
low.defvjp(low_keep, low_pass)
low_back.defvjp(back_keep, back_low)
epsilon = 1e-05
theta_base = 10000.0
masked_value = -1e+30
highest = lax.Precision.HIGHEST

def rope_tables(segment_ids):
    documents = jnp.arange(DOCS, dtype=jnp.int32)
    member = (segment_ids[:, :, None] == documents[None, None, :]).astype(jnp.int32)
    doc_sizes = lax.optimization_barrier(jnp.sum(member, axis=1))
    earlier = (documents[None, None, :] < segment_ids[:, :, None]).astype(jnp.int32)
    first_token = lax.optimization_barrier(jnp.sum(earlier * doc_sizes[:, None, :], axis=-1))
    place = jnp.arange(segment_ids.shape[1], dtype=jnp.int32)[None, :] - first_token
    half_dim = HD // 2
    frequency = theta_base ** (-2.0 * jnp.arange(half_dim, dtype=jnp.float32) / HD)
    angle = place.astype(jnp.float32)[:, :, None] * frequency[None, None, :]
    angle = jnp.concatenate([angle, angle], axis=-1)
    return (jnp.cos(angle), jnp.sin(angle))

def rotate(values, cosine, sine_table):
    half_dim = values.shape[-1] // 2
    turned = jnp.concatenate([-values[..., half_dim:], values[..., :half_dim]], axis=-1)
    return values * cosine[:, :, None, :] + turned * sine_table[:, :, None, :]

def normalize(values, gain):
    inverse = lax.rsqrt(lax.optimization_barrier(jnp.mean(values * values, axis=-1, keepdims=True)) + epsilon)
    return values * inverse * gain

def block_mask(seg_row, block_start, block_rows):
    query_seg = lax.dynamic_slice_in_dim(seg_row, block_start, block_rows, 0)
    query_place = block_start + jnp.arange(block_rows, dtype=jnp.int32)
    key_place = jnp.arange(seg_row.shape[0], dtype=jnp.int32)
    return (key_place[None, :] <= query_place[:, None]) & (query_seg[:, None] == seg_row[None, :])

def score_block(block_query, owner_index, block_start, keys, value_all, seg_rows):
    block_rows = block_query.shape[0]
    key_rows = lax.dynamic_index_in_dim(keys, owner_index, 0, keepdims=False)
    value_rows = lax.dynamic_index_in_dim(value_all, owner_index, 0, keepdims=False)
    seg_row = lax.dynamic_index_in_dim(seg_rows, owner_index, 0, keepdims=False)
    allowed = block_mask(seg_row, block_start, block_rows)
    scores = low_back(jnp.einsum('qhd,khd->hqk', block_query, key_rows, precision=highest) * HD ** (-0.5))
    masked = jnp.where(allowed[None], scores, masked_value)
    weights_low = low(jax.nn.softmax(masked, axis=-1))
    return jnp.einsum('hqk,khd->qhd', weights_low, value_rows, precision=highest).reshape(block_rows, D)

def attention(query, keys, value_all, seg_rows):
    batch_size = query.shape[0]
    block_rows = min(512, SEQ_LEN)
    blocks = SEQ_LEN // block_rows
    query_blocks = query.reshape(batch_size * blocks, block_rows, H, HD)
    owners = jnp.repeat(jnp.arange(batch_size, dtype=jnp.int32), blocks)
    starts = jnp.tile(jnp.arange(blocks, dtype=jnp.int32) * block_rows, batch_size)
    checked = jax.checkpoint(score_block)
    mapped_out = lax.map(lambda mapped: checked(mapped[0], mapped[1], mapped[2], keys, value_all, seg_rows), (query_blocks, owners, starts))
    return mapped_out.reshape(batch_size, SEQ_LEN, D)

def layer(start_x, weights_f32, cosine, sine_table, seg_rows):
    norm_attn, norm_mlp, w_query, w_key, w_value, w_out, w_gate, w_up, w_down = weights_f32
    batch_size = start_x.shape[0]
    head_shape = (batch_size, SEQ_LEN, H, HD)
    normed_attn = low(normalize(start_x, norm_attn))
    query_lin = low_back(jnp.dot(normed_attn, w_query, precision=highest)).reshape(head_shape)
    key_lin = low_back(jnp.dot(normed_attn, w_key, precision=highest)).reshape(head_shape)
    value_all = low(low_back(jnp.dot(normed_attn, w_value, precision=highest))).reshape(head_shape)
    query = low(low_back(rotate(query_lin, cosine, sine_table)))
    keys = low(low_back(rotate(key_lin, cosine, sine_table)))
    mixed = low(low_back(attention(query, keys, value_all, seg_rows)))
    middle = start_x + low_back(jnp.dot(mixed, w_out, precision=highest))
    normed_mlp = low(normalize(middle, norm_mlp))
    gate_value = low_back(jnp.dot(normed_mlp, w_gate, precision=highest))
    up_value = low_back(jnp.dot(normed_mlp, w_up, precision=highest))
    hidden = low(jax.nn.silu(gate_value) * up_value)
    return middle + low_back(jnp.dot(hidden, w_down, precision=highest))

def reference(inputs, segment_ids, cotangent, norm_attn, norm_mlp, w_query, w_key, w_value, w_out, w_gate, w_up, w_down):
    params = (norm_attn, norm_mlp, w_query, w_key, w_value, w_out, w_gate, w_up, w_down)
    params = tuple((weight.astype(jnp.float32) for weight in params))
    cosine, sine_table = rope_tables(segment_ids)
    pairs = SEQS // 2

    def regroup(array):
        return array.reshape((pairs, 2) + array.shape[1:])

    def accumulate(totals, element):
        rows_in, grad_rows, cos_rows, sin_rows, seg_rows = element

        def forward(start_x, *weights_f32):
            return layer(start_x, weights_f32, cos_rows, sin_rows, seg_rows)
        result, pullback = jax.vjp(forward, rows_in.astype(jnp.float32), *params)
        grads = pullback(grad_rows.astype(jnp.float32))
        totals = tuple((total + grad for total, grad in zip(totals, grads[1:])))
        return (totals, (result.astype(jnp.bfloat16), grads[0]))
    empty = tuple((jnp.zeros(weight.shape, jnp.float32) for weight in params))
    totals, (outputs, input_grads) = lax.scan(accumulate, empty, (regroup(inputs), regroup(cotangent), regroup(cosine), regroup(sine_table), regroup(segment_ids)))
    whole_shape = (SEQS, SEQ_LEN, D)
    return (outputs.reshape(whole_shape), input_grads.reshape(whole_shape), totals[0], totals[1], totals[2], totals[3], totals[4], totals[5], totals[6], totals[7], totals[8])
```

```python
import functools

import jax
import jax.numpy as jnp
from jax import lax
from jax.experimental import pallas as pl
from jax.experimental.pallas import tpu as pltpu
from jax.sharding import PartitionSpec as P

HD = 64
DOCS = 7
epsilon = 1e-05
theta_base = 10000.0
masked_value = -1e30
MESH = pl.DeviceIdType.MESH
f32 = jnp.float32
bf16 = jnp.bfloat16
QB = 256
MB = 256


def dot(left, right, left_dim, right_dim):
    return lax.dot_general(
        left, right, (((left_dim,), (right_dim,)), ((), ())), preferred_element_type=f32
    )


def strip_offset(block):
    return QB * block * (block + 1) // 2


def fold_rows(values):
    rows, width = values.shape
    return jnp.sum(values.reshape(rows // 8, 8, width), axis=0)


def block_kernel(
    G, S, T, L, D, FF,
    x, seg, cot, gain_a, gain_m, wq, wk, wv, wo, wg, wu, wd,
    out, gin, g_ga, g_gm, g_qkv, g_out, g_gate, g_up, g_down,
    xs, cots, seg_other, first_s, cos_s, sin_s, n_s, wqkv, wqkvT, wo_s, wg_s, wu_s, wd_s,
    qTz, k_s, kT, v_s, vT, p_s, inv_tot, mixT, mfull, mid, nm, hid, dga, dup, da, dmT, outb,
    dO_in, dOz, dacc_k, dacc_v, dn_in,
    w_sem, loc_sem, seg_sem, x_send, x_recv, fwd_send, cot_send, cot_recv, mix_send, mix_recv,
    out_send, out_recv, dm_send, dm_recv, dn_send, dn_recv, gin_send, gin_recv, g_sem,
):
    d = lax.axis_index("dp")
    z = lax.axis_index("seq")
    c = lax.rem(d, 2)
    pair = d - c
    sib = pair + 1 - c
    gz = z // G
    lz = lax.rem(z, G)
    half = L // 2
    Dh = D // 2
    NH = Dh // HD

    def remote(src, dst, send, recv, dp, seq):
        return pltpu.make_async_remote_copy(
            src_ref=src, dst_ref=dst, send_sem=send, recv_sem=recv,
            device_id=(dp, seq), device_id_type=MESH,
        )

    loads = [
        pltpu.make_async_copy(w.at[:, pl.ds(pl.multiple_of(c * Dh, Dh), Dh)], wqkv.at[i], w_sem.at[i])
        for i, w in enumerate((wq, wk, wv))
    ] + [
        pltpu.make_async_copy(w, s, w_sem.at[3 + i])
        for i, (w, s) in enumerate(((wo, wo_s), (wg, wg_s), (wu, wu_s), (wd, wd_s)))
    ]
    for load in loads:
        load.start()

    barrier = pltpu.get_barrier_semaphore()
    for step in range(1, 2 * S):
        other = lax.rem(c * S + z + step, 2 * S)
        pl.semaphore_signal(
            barrier, inc=1, device_id=(pair + other // S, lax.rem(other, S)), device_id_type=MESH
        )
    pl.semaphore_wait(barrier, 2 * S - 1)

    seg_copy = remote(seg, seg_other, seg_sem.at[0], seg_sem.at[1], sib, z)
    seg_copy.start()

    def x_rows(index):
        return xs.at[pl.ds(pl.multiple_of(index * T, T), T)]

    def x_copy(l):
        return remote(x.at[l], x_rows(z), x_send.at[l], x_recv.at[z], d, c * G + l)

    own_x = pltpu.make_async_copy(x.at[lz], x_rows(z), loc_sem.at[0])
    own_fwd = remote(x.at[lz], x_rows(z), fwd_send.at[0], x_recv.at[z], sib, z)

    @pl.when(gz == c)
    def _():
        own_x.start()
        own_fwd.start()

    for l in range(G):
        @pl.when(c * G + l != z)
        def _():
            x_copy(l).start()

    for load in loads:
        load.wait()
    for i in range(3):
        wqkvT[i * Dh:(i + 1) * Dh, :] = wqkv[i].T
    seg_copy.wait()
    seg_mine = jnp.where(gz == c, seg[...], seg_other[...])
    row = jnp.zeros((1, L), jnp.int32)
    for l in range(G):
        row = jnp.where(lz == l, seg_mine[l:l + 1, :], row)
    ids = row.astype(f32)
    first = jnp.zeros((1, L), f32)
    for doc in range(1, DOCS):
        before = jnp.sum(jnp.where(ids < doc, 1.0, 0.0), axis=1, keepdims=True)
        first = jnp.where(ids >= doc, before, first)
    first_s[...] = jnp.broadcast_to(first, (8, L))
    token = lax.broadcasted_iota(jnp.int32, (1, L), 1).astype(f32)
    place = token - first
    order = lax.broadcasted_iota(jnp.int32, (HD // 2, 1), 0).astype(f32)
    frequency = jnp.exp(order * f32(-2.0 * 9.210340371976184 / HD))
    angle = place * frequency
    cos_s[...] = jnp.cos(angle)
    sin_s[...] = jnp.sin(angle)

    def rms(values):
        inverse = lax.rsqrt(jnp.mean(values * values, axis=-1, keepdims=True) + epsilon)
        return values * inverse, inverse

    def project(start, size):
        rows = pl.ds(start, size)
        plain, _ = rms(xs[rows, :].astype(f32))
        normed = (plain * gain_a[...]).astype(bf16)
        n_s[rows, :] = normed
        lin = dot(wqkvT[...], normed, 1, 1)
        cosine, sine = cos_s[:, rows], sin_s[:, rows]

        def rotated(base, scale):
            parts = []
            for h in range(NH):
                a = lin[base + h * HD:base + h * HD + HD // 2]
                b = lin[base + h * HD + HD // 2:base + (h + 1) * HD]
                parts.append(jnp.concatenate([a * cosine - b * sine, b * cosine + a * sine], axis=0))
            return parts

        zeros = jnp.zeros((HD, size), bf16)
        for h, q in enumerate(rotated(0, 1.0)):
            q = (q.astype(bf16).astype(f32) * HD ** -0.5).astype(bf16)
            qTz[h, :, rows] = jnp.concatenate([q, zeros] if h % 2 == 0 else [zeros, q], axis=0)
        keys = jnp.concatenate(rotated(Dh, 1.0), axis=0).astype(bf16)
        kT[:, rows] = keys
        k_s[rows, :] = keys.T
        values = lin[2 * Dh:].astype(bf16)
        vT[:, rows] = values
        v_s[rows, :] = values.T

    for step in range(S):
        source = lax.rem(z + step, S)
        arrived = remote(x.at[0], x_rows(source), x_send.at[0], x_recv.at[source], sib, z)
        if step == 0:
            @pl.when(gz == c)
            def _():
                own_x.wait()

            @pl.when(gz != c)
            def _():
                arrived.wait_recv()
        else:
            arrived.wait_recv()

            @pl.when(gz == c)
            def _():
                remote(x_rows(source), x_rows(source), fwd_send.at[step], x_recv.at[source], sib, z).start()

        @pl.loop(0, T // QB)
        def _(i):
            project(pl.multiple_of(source * T + i * QB, QB), QB)

    for l in range(G):
        @pl.when(c * G + l != z)
        def _():
            x_copy(l).wait_send()

    @pl.when(gz == c)
    def _():
        own_fwd.wait_send()
        for step in range(1, S):
            remote(x.at[0], x_rows(z), fwd_send.at[step], x_recv.at[z], sib, z).wait_send()

    to_core = z // G
    slot = lax.rem(z, G)

    def cot_rows(index):
        return cots.at[pl.ds(pl.multiple_of(index * T, T), T)]

    def cot_copy(l):
        return remote(cot.at[l], cot_rows(slot), cot_send.at[l], cot_recv.at[slot], pair + to_core, c * G + l)

    own_cot = pltpu.make_async_copy(cot.at[lz], cot_rows(slot), loc_sem.at[1])
    keeps_own = (gz == c) & (to_core == c)
    for l in range(G):
        here = (c * G + l == z) & (to_core == c)

        @pl.when(jnp.logical_not(here))
        def _():
            cot_copy(l).start()

    @pl.when(keeps_own)
    def _():
        own_cot.start()

    def mask_of(strip_rows, qb, s, row0):
        j = (lax.broadcasted_iota(jnp.int32, (strip_rows, QB), 0) + row0).astype(f32)
        i = (lax.broadcasted_iota(jnp.int32, (1, QB), 1) + qb * QB).astype(f32)
        begin = first_s[0:1, qb * QB:(qb + 1) * QB]
        return jnp.where((j >= begin) & (j <= i), s, masked_value)

    def mix_copy(h):
        return remote(
            mixT.at[pl.ds(pl.multiple_of(h * HD, HD), HD), pl.ds(pl.multiple_of((1 - c) * half, half), half)],
            mfull.at[pl.ds(pl.multiple_of(c * Dh + h * HD, HD), HD), :],
            mix_send.at[h], mix_recv.at[h], sib, z,
        )

    NQ = L // QB

    @pl.loop(0, NH)
    def _(h):
        rows = pl.ds(pl.multiple_of(h * HD, HD), HD)
        lanes = pl.ds(pl.multiple_of((h // 2) * 2 * HD, 2 * HD), 2 * HD)
        for qb in range(NQ):
            cols = slice(qb * QB, (qb + 1) * QB)
            depth = (qb + 1) * QB
            s = dot(k_s[0:depth, lanes], qTz[h, :, cols], 1, 0)
            if qb == NQ - 1:
                s = mask_of(depth, qb, s, 0)
            elif qb < 2:
                s = mask_of(depth, qb, s, 0)
            else:
                s = jnp.concatenate(
                    [mask_of(QB, qb, s[:QB], 0), s[QB:depth - QB], mask_of(QB, qb, s[depth - QB:], depth - QB)],
                    axis=0,
                )
            top = jnp.max(s, axis=0, keepdims=True)
            expanded = jnp.exp(s - top)
            inverse = 1.0 / jnp.sum(expanded, axis=0, keepdims=True)
            low = expanded.astype(bf16)
            p_s[h, strip_offset(qb):strip_offset(qb) + depth, :] = low
            inv_tot[h, :, cols] = jnp.broadcast_to(inverse, (8, QB))
            mixT[rows, cols] = (dot(vT[rows, 0:depth], low, 1, 0) * inverse).astype(bf16)
        mix_copy(h).start()
        mfull[pl.ds(pl.multiple_of(c * Dh + h * HD, HD), HD), :] = mixT[
            rows, pl.ds(pl.multiple_of(c * half, half), half)
        ]

    @pl.loop(0, NH)
    def _(h):
        mix_copy(h).wait_send()
        remote(
            mixT.at[0:HD, 0:half], mfull.at[pl.ds(pl.multiple_of((1 - c) * Dh + h * HD, HD), HD), :],
            mix_send.at[h], mix_recv.at[h], sib, z,
        ).wait_recv()

    for l in range(G):
        here = (c * G + l == z) & (to_core == c)

        @pl.when(jnp.logical_not(here))
        def _():
            cot_copy(l).wait_send()

    for j in range(G):
        mine = (gz == c) & (c * G + j == z)

        @pl.when(jnp.logical_not(mine))
        def _():
            remote(cot.at[0], cot_rows(j), cot_send.at[0], cot_recv.at[j], sib, z).wait_recv()

    @pl.when(keeps_own)
    def _():
        own_cot.wait()

    middle_col = (FF // 2 + 255) // 256 * 256
    ff_cuts = ((0, middle_col), (middle_col, FF))
    g_gm[...] = jnp.zeros((8, D), f32)

    @pl.loop(0, half // MB)
    def _(i):
        start = pl.multiple_of(i * MB, MB)
        rows = pl.ds(start, MB)
        base = xs[pl.ds(pl.multiple_of(c * half + start, MB), MB), :].astype(f32)
        middle = base + dot(mfull[:, rows], wo_s[...], 0, 0)
        plain, inverse = rms(middle)
        gain = gain_m[...]
        normed = (plain * gain).astype(bf16)
        nm[rows, :] = normed
        grad = cots[rows, :]
        result = middle
        d_normed = None
        for first_col, last_col in ff_cuts:
            cut = slice(first_col, last_col)
            gate = dot(normed, wg_s[:, cut], 1, 0)
            up = dot(normed, wu_s[:, cut], 1, 0)
            sig = 1.0 / (1.0 + jnp.exp(-gate))
            act = gate * sig
            hidden = (act * up).astype(bf16)
            hid[rows, cut] = hidden
            result = result + dot(hidden, wd_s[cut, :], 1, 0)
            d_hidden = dot(grad, wd_s[cut, :], 1, 1)
            d_gate = (d_hidden * up * sig * (1.0 + gate * (1.0 - sig))).astype(bf16)
            d_up = (d_hidden * act).astype(bf16)
            dga[rows, cut] = d_gate
            dup[rows, cut] = d_up
            term = dot(d_gate, wg_s[:, cut], 1, 1) + dot(d_up, wu_s[:, cut], 1, 1)
            d_normed = term if d_normed is None else d_normed + term
        outb[rows, :] = result.astype(bf16)
        scaled = d_normed * gain
        g_gm[...] += fold_rows(d_normed * plain)
        d_middle = grad.astype(f32) + inverse * (scaled - plain * jnp.mean(scaled * plain, axis=-1, keepdims=True))
        mid[rows, :] = d_middle
        d_attn = d_middle.astype(bf16)
        da[rows, :] = d_attn
        dmT[:, rows] = dot(wo_s[...], d_attn, 1, 1).astype(bf16)

    dm_copy = remote(
        dmT.at[pl.ds(pl.multiple_of((1 - c) * Dh, Dh), Dh), :], dO_in, dm_send.at[0], dm_recv.at[0], sib, z
    )
    dm_copy.start()

    def back_copy(j, src, dst, send, recv):
        return remote(src.at[pl.ds(j * T, T)], dst.at[lz], send.at[j], recv.at[lz], pair + gz, c * G + j)

    def back_start(src, dst, send, recv, local):
        for j in range(G):
            mine = (gz == c) & (c * G + j == z)

            @pl.when(jnp.logical_not(mine))
            def _():
                back_copy(j, src, dst, send, recv).start()

            @pl.when(mine)
            def _():
                pltpu.make_async_copy(src.at[pl.ds(j * T, T)], dst.at[lz], local).start()

    def back_wait(src, dst, send, recv, local):
        for j in range(G):
            mine = (gz == c) & (c * G + j == z)

            @pl.when(jnp.logical_not(mine))
            def _():
                back_copy(j, src, dst, send, recv).wait_send()

            @pl.when(mine)
            def _():
                pltpu.make_async_copy(src.at[pl.ds(j * T, T)], dst.at[lz], local).wait()
        for l in range(G):
            mine = (c * G + l == z) & (z // G == c)

            @pl.when(jnp.logical_not(mine))
            def _():
                remote(src.at[pl.ds(0, T)], dst.at[l], send.at[0], recv.at[l], sib, z).wait_recv()

    back_start(outb, out, out_send, out_recv, loc_sem.at[2])

    wg_s[...] = dot(nm[...], dga[...], 0, 0).astype(bf16)
    wu_s[...] = dot(nm[...], dup[...], 0, 0).astype(bf16)
    wd_s[...] = dot(hid[...], cots[...], 0, 0).astype(bf16)
    wo_s[...] = dot(mfull[...], da[...], 1, 0).astype(bf16)
    copies = [
        pltpu.make_async_copy(wg_s, g_gate, g_sem.at[0]),
        pltpu.make_async_copy(wu_s, g_up, g_sem.at[1]),
        pltpu.make_async_copy(wd_s, g_down, g_sem.at[2]),
        pltpu.make_async_copy(wo_s, g_out, g_sem.at[3]),
    ]
    for copy in copies:
        copy.start()

    dm_copy.wait()

    def take(values, offset):
        tokens = values.shape[1]
        zeros = jnp.zeros((HD, tokens), bf16)
        for h in range(NH):
            inverse = inv_tot[h, 0:1, pl.ds(offset, tokens)]
            grad = (values[h * HD:(h + 1) * HD].astype(f32) * inverse).astype(bf16)
            dOz[h, :, pl.ds(offset, tokens)] = jnp.concatenate(
                [grad, zeros] if h % 2 == 0 else [zeros, grad], axis=0
            )

    take(dmT[pl.ds(pl.multiple_of(c * Dh, Dh), Dh), :], pl.multiple_of(c * half, half))
    take(dO_in[...], pl.multiple_of((1 - c) * half, half))

    parts = (dga, dup, hid)

    def unrotated(values, cosine, sine):
        a, b = values[:HD // 2], values[HD // 2:]
        return jnp.concatenate([a * cosine + b * sine, b * cosine - a * sine], axis=0)

    @pl.loop(0, NH)
    def _(h):
        rows = pl.ds(pl.multiple_of(h * HD, HD), HD)
        lanes = pl.ds(pl.multiple_of((h // 2) * 2 * HD, 2 * HD), 2 * HD)
        inner = pl.ds(pl.multiple_of(lax.rem(h, 2) * HD, HD), HD)
        for qb in reversed(range(NQ)):
            cols = slice(qb * QB, (qb + 1) * QB)
            depth = (qb + 1) * QB
            low = p_s[h, strip_offset(qb):strip_offset(qb) + depth, :]
            grad = dOz[h, inner, cols]
            delta = jnp.sum(grad.astype(f32) * mixT[rows, cols].astype(f32), axis=0, keepdims=True)
            d_probs = dot(v_s[0:depth, lanes], dOz[h, :, cols], 1, 0)
            d_scores = (low.astype(f32) * (d_probs - delta)).astype(bf16)
            add_v = dot(grad, low, 1, 1)
            add_k = dot(qTz[h, inner, cols], d_scores, 1, 1)
            if qb == NQ - 1:
                dacc_v[:, 0:depth] = add_v
                dacc_k[:, 0:depth] = add_k
            else:
                dacc_v[:, 0:depth] += add_v
                dacc_k[:, 0:depth] += add_k
            d_query = dot(kT[rows, 0:depth], d_scores, 1, 0) * HD ** -0.5
            side, lane = divmod(qb * QB, half)
            parts[0][pl.ds(pl.multiple_of(side * Dh + h * HD, HD), HD), lane:lane + QB] = unrotated(
                d_query.astype(bf16).astype(f32), cos_s[:, cols], sin_s[:, cols]
            ).astype(bf16)
        for side in range(2):
            cols = slice(side * half, (side + 1) * half)
            place_rows = pl.ds(pl.multiple_of(side * Dh + h * HD, HD), HD)
            parts[1][place_rows, 0:half] = unrotated(
                dacc_k[:, cols].astype(bf16).astype(f32), cos_s[:, cols], sin_s[:, cols]
            ).astype(bf16)
            parts[2][place_rows, 0:half] = dacc_v[:, cols].astype(bf16)

    back_wait(outb, out, out_send, out_recv, loc_sem.at[2])

    def back_norm(side, start):
        side_rows = pl.ds(pl.multiple_of(side * Dh, Dh), Dh)
        total = None
        for i in range(3):
            term = dot(parts[i][side_rows, pl.ds(start, MB)], wqkvT[i * Dh:(i + 1) * Dh, :], 0, 0)
            total = term if total is None else total + term
        return total

    @pl.loop(0, half // MB)
    def _(i):
        start = pl.multiple_of(i * MB, MB)
        da[pl.ds(start, MB), :] = back_norm(1 - c, start).astype(bf16)

    dn_copy = remote(da, dn_in, dn_send.at[0], dn_recv.at[0], sib, z)
    dn_copy.start()

    for i in range(3):
        grad = dot(parts[i][0:Dh, 0:half], n_s[0:half, :], 1, 0)
        grad = grad + dot(parts[i][Dh:2 * Dh, 0:half], n_s[half:L, :], 1, 0)
        wqkv[i] = grad.T.astype(bf16)
    copies.append(pltpu.make_async_copy(wqkv, g_qkv, g_sem.at[4]))
    copies[-1].start()
    dn_copy.wait()

    g_ga[...] = jnp.zeros((8, D), f32)

    @pl.loop(0, half // MB)
    def _(i):
        start = pl.multiple_of(i * MB, MB)
        rows = pl.ds(start, MB)
        own = pl.ds(pl.multiple_of(c * half + start, MB), MB)
        d_normed = back_norm(c, start) + dn_in[rows, :].astype(f32)
        plain, inverse = rms(xs[own, :].astype(f32))
        scaled = d_normed * gain_a[...]
        g_ga[...] += fold_rows(d_normed * plain)
        d_start = inverse * (scaled - plain * jnp.mean(scaled * plain, axis=-1, keepdims=True))
        nm[rows, :] = (mid[rows, :] + d_start).astype(bf16)

    back_start(nm, gin, gin_send, gin_recv, loc_sem.at[3])
    for copy in copies:
        copy.wait()
    back_wait(nm, gin, gin_send, gin_recv, loc_sem.at[3])


def on_device(
    G, S,
    inputs, segment_ids, cotangent, norm_attn, norm_mlp, w_query, w_key, w_value, w_out, w_gate, w_up, w_down,
):
    _, T, D = inputs.shape
    FF = w_gate.shape[1]
    L = T * S
    half, Dh = L // 2, D // 2
    NH = Dh // HD
    anywhere = pl.BlockSpec(memory_space=pl.ANY)
    vmem = pl.BlockSpec(memory_space=pltpu.VMEM)
    dma = pltpu.SemaphoreType.DMA

    def buf(*shape, dtype=bf16):
        return pltpu.VMEM(shape, dtype)

    strips = strip_offset(L // QB)
    outs = pl.pallas_call(
        functools.partial(block_kernel, G, S, T, L, D, FF),
        out_shape=[
            jax.ShapeDtypeStruct((G, T, D), bf16),
            jax.ShapeDtypeStruct((G, T, D), bf16),
            jax.ShapeDtypeStruct((8, D), f32),
            jax.ShapeDtypeStruct((8, D), f32),
            jax.ShapeDtypeStruct((3, D, Dh), bf16),
            jax.ShapeDtypeStruct((D, D), bf16),
            jax.ShapeDtypeStruct((D, FF), bf16),
            jax.ShapeDtypeStruct((D, FF), bf16),
            jax.ShapeDtypeStruct((FF, D), bf16),
        ],
        in_specs=[anywhere, vmem, anywhere, vmem, vmem] + [anywhere] * 7,
        out_specs=[anywhere, anywhere, vmem, vmem] + [anywhere] * 5,
        scratch_shapes=[
            buf(L, D), buf(half, D), buf(G, L, dtype=jnp.int32), buf(8, L, dtype=f32),
            buf(HD // 2, L, dtype=f32), buf(HD // 2, L, dtype=f32),
            buf(L, D), buf(3, D, Dh), buf(3 * Dh, D), buf(D, D), buf(D, FF), buf(D, FF), buf(FF, D),
            buf(NH, 2 * HD, L), buf(L, Dh), buf(Dh, L), buf(L, Dh), buf(Dh, L),
            buf(NH, strips, QB), buf(NH, 8, L, dtype=f32), buf(Dh, L), buf(D, half),
            buf(half, D, dtype=f32), buf(half, D), buf(half, FF), buf(half, FF), buf(half, FF),
            buf(half, D), buf(D, half), buf(half, D),
            buf(Dh, half), buf(NH, 2 * HD, L), buf(HD, L, dtype=f32), buf(HD, L, dtype=f32),
            buf(half, D),
            dma((7,)), dma((4,)), dma((2,)), dma((G,)), dma((S,)), dma((S,)), dma((G,)), dma((G,)),
            dma((NH,)), dma((NH,)), dma((G,)), dma((G,)), dma((1,)), dma((1,)), dma((1,)), dma((1,)),
            dma((G,)), dma((G,)), dma((5,)),
        ],
        compiler_params=pltpu.CompilerParams(
            collective_id=0, has_side_effects=True, vmem_limit_bytes=63 * 2**20
        ),
    )(
        inputs, segment_ids, cotangent, norm_attn.reshape(1, D), norm_mlp.reshape(1, D),
        w_query, w_key, w_value, w_out, w_gate, w_up, w_down,
    )
    out, gin, g_ga, g_gm, g_qkv, g_out, g_gate, g_up, g_down = outs
    c = lax.rem(lax.axis_index("dp"), 2)

    def whole(part):
        return lax.dynamic_update_slice(jnp.zeros((D, D), f32), part.astype(f32), (0, c * Dh))

    grads = (
        jnp.sum(g_ga, axis=0), jnp.sum(g_gm, axis=0),
        whole(g_qkv[0]), whole(g_qkv[1]), whole(g_qkv[2]),
        g_out.astype(f32), g_gate.astype(f32), g_up.astype(f32), g_down.astype(f32),
    )
    return (out, gin.astype(f32)) + tuple(lax.psum(grads, ("dp", "seq")))


def solution(mesh):
    S = mesh.shape["seq"]
    G = S // 2
    rows = P("dp", "seq", None)
    return jax.shard_map(
        functools.partial(on_device, G, S),
        mesh=mesh,
        in_specs=(rows, P("dp", None), rows) + (P(),) * 9,
        out_specs=(rows, rows) + (P(),) * 9,
        check_vma=False,
    )
```

```python
import functools

import jax
import jax.numpy as jnp
from jax import lax
from jax.experimental import pallas as pl
from jax.experimental.pallas import tpu as pltpu
from jax.sharding import PartitionSpec as P

HD = 64
DOCS = 7
epsilon = 1e-05
theta_base = 10000.0
masked_value = -1e30
MESH = pl.DeviceIdType.MESH
f32 = jnp.float32
bf16 = jnp.bfloat16
QB = 256
MB = 256
EDGE = 128


def dot(left, right, left_dim, right_dim):
    return lax.dot_general(
        left, right, (((left_dim,), (right_dim,)), ((), ())), preferred_element_type=f32
    )


def strip_offset(block):
    return QB * block * (block + 1) // 2


def padded(rows, shards):
    unit = 16 * shards
    return (rows + unit - 1) // unit * unit


class Total:
    def __init__(self, NP, S, place, remote, buf, result, local, base, count, land_s, land_p, land_z, send, recv):
        self.NP, self.S = NP, S
        self.base, self.count = base, count
        self.result, self.local = result, local
        self.c, self.pr, self.z, self.own, self.other = place
        self.remote = remote
        self.buf, self.land_s, self.land_p, self.land_z = buf, land_s, land_p, land_z
        self.send, self.recv = send, recv
        self.part = count // NP
        self.shard = self.part // S

    def rows(self, pr, z=None):
        if z is None:
            return pl.ds(pl.multiple_of(self.base + pr * self.part, 16), self.part)
        return pl.ds(pl.multiple_of(self.base + pr * self.part + z * self.shard, 16), self.shard)

    def copy(self, src, dst, index, pr, z, c):
        return self.remote(src, dst, self.send.at[index], self.recv.at[index], 2 * pr + c, z)

    def core_scatter(self):
        return [self.copy(self.buf.at[pl.ds(self.base, self.count), self.other], self.land_s, 0, self.pr, self.z, 1 - self.c)]

    def core_gather(self):
        half = self.result.at[pl.ds(self.base, self.count), self.own]
        return [self.copy(half, half, 1, self.pr, self.z, 1 - self.c)]

    def pair_scatter(self):
        copies = []
        for k in range(1, self.NP):
            to = lax.rem(self.pr + k, self.NP)
            src = self.buf.at[self.rows(to), self.own]
            copies.append(self.copy(src, self.land_p.at[k - 1], 1 + k, to, self.z, self.c))
        return copies

    def pair_gather(self):
        copies = []
        for k in range(1, self.NP):
            to = lax.rem(self.pr + k, self.NP)
            src = self.result.at[self.rows(self.pr), self.own]
            copies.append(self.copy(src, src, self.NP + k, to, self.z, self.c))
        return copies

    def z_scatter(self):
        copies = []
        for k in range(1, self.S):
            to = lax.rem(self.z + k, self.S)
            src = self.buf.at[self.rows(self.pr, to), self.own]
            copies.append(self.copy(src, self.land_z.at[k - 1], 2 * self.NP - 1 + k, self.pr, to, self.c))
        return copies

    def z_gather(self):
        copies = []
        for k in range(1, self.S):
            to = lax.rem(self.z + k, self.S)
            rows = self.rows(self.pr, self.z)
            src, dst = self.buf.at[rows, self.own], self.result.at[rows, self.own]
            copies.append(self.copy(src, dst, 2 * self.NP + self.S - 2 + k, self.pr, to, self.c))
        return copies

    def keep(self):
        rows = self.rows(self.pr, self.z)
        return pltpu.make_async_copy(self.buf.at[rows, self.own], self.result.at[rows, self.own], self.local)

    @staticmethod
    def start(copies):
        for copy in copies:
            copy.start()

    @staticmethod
    def wait(copies):
        for copy in copies:
            copy.wait()

    def add(self, first, count, lands):
        size = self.shard

        @pl.loop(0, count)
        def _(i):
            rows = pl.ds(pl.multiple_of(self.base + first + i * size, 16), size)
            total = self.buf[rows, self.own].astype(f32)
            for land in lands:
                total = total + land[pl.ds(pl.multiple_of(i * size, 16), size), :].astype(f32)
            self.buf[rows, self.own] = total.astype(bf16)

    def core_add(self):
        self.wait(self.core_scatter())
        self.add(0, self.NP * self.S, [self.land_s])
        self.start(self.pair_scatter())

    def pair_add(self):
        self.wait(self.pair_scatter())
        self.add(self.pr * self.part, self.S, [self.land_p.at[k] for k in range(self.NP - 1)])
        self.start(self.z_scatter())

    def z_add(self):
        self.wait(self.z_scatter())
        self.add(self.pr * self.part + self.z * self.shard, 1, [self.land_z.at[k] for k in range(self.S - 1)])
        self.start([self.keep()] + self.z_gather())

    def z_done(self):
        self.wait([self.keep()] + self.z_gather())
        self.start(self.pair_gather())

    def pair_done(self):
        self.wait(self.pair_gather())
        self.start(self.core_gather())

    def core_done(self):
        self.wait(self.core_gather())


def fold_rows(values):
    rows, width = values.shape
    return jnp.sum(values.reshape(rows // 8, 8, width), axis=0)


def split_rows(rows, first, shards):
    unit = 16 * shards
    units = rows // unit
    head = first // unit
    mid = (units - head + 1) // 2
    return head * unit, mid * unit, (units - head - mid) * unit


def interleave(main, count_main, side, count_side):
    steps = max(count_main, count_side)
    done_main = done_side = 0
    for step in range(1, steps + 1):
        while done_main < step * count_main / steps:
            next(main, None)
            done_main += 1
        while done_side < step * count_side / steps:
            next(side, None)
            done_side += 1
    for _ in main:
        pass
    for _ in side:
        pass


def block_kernel(
    G, S, NP, T, L, D, FF,
    x, seg, cot, gain_a, gain_m, wq, wk, wv, wo, wgT, wuT, wd,
    out, gin, out_a, out_b,
    xs, cots, seg_other, first_s, cos_s, sin_s, n_s, wqkvT, gA, gB,
    qT, kT, vT, p_s, s_buf, inv_tot, mixT, mfull, nm, hid, dga, dup, da, dmT,
    dOT, dacc_k, dacc_v, g_ga, g_gm,
    land_s1, land_p1, land_z1, land_s2, land_p2, land_z2, land_s3, land_p3, land_z3, land_p4, land_z4,
    w_sem, loc_sem, seg_sem, x_send, x_recv, fwd_send, cot_send, cot_recv, mix_send, mix_recv,
    out_send, out_recv, dm_send, dm_recv, dn_send, dn_recv, gin_send, gin_recv, g_sem,
    t1_send, t1_recv, t2_send, t2_recv, t3_send, t3_recv, t4_send, t4_recv,
):
    d = lax.axis_index("dp")
    z = lax.axis_index("seq")
    c = lax.rem(d, 2)
    pair = d - c
    sib = pair + 1 - c
    gz = z // G
    lz = lax.rem(z, G)
    half = L // 2
    Dh = D // 2
    NH = Dh // HD

    def remote(src, dst, send, recv, dp, seq):
        return pltpu.make_async_remote_copy(
            src_ref=src, dst_ref=dst, send_sem=send, recv_sem=recv,
            device_id=(dp, seq), device_id_type=MESH,
        )

    own_cols = pl.ds(pl.multiple_of(c * Dh, Dh), Dh)
    other_cols = pl.ds(pl.multiple_of((1 - c) * Dh, Dh), Dh)
    pr = d // 2
    here_at = (c, pr, z, own_cols, other_cols)
    RA = gA.shape[0]
    count_1, count_2, count_3 = split_rows(RA, FF, NP * S)
    sum_1 = Total(
        NP, S, here_at, remote, gA, out_a, g_sem.at[0], 0, count_1, land_s1, land_p1, land_z1, t1_send, t1_recv
    )
    sum_2 = Total(
        NP, S, here_at, remote, gA, out_a, g_sem.at[1], count_1, count_2,
        land_s2, land_p2, land_z2, t2_send, t2_recv,
    )
    sum_3 = Total(
        NP, S, here_at, remote, gA, out_a, g_sem.at[2], count_1 + count_2, count_3,
        land_s3, land_p3, land_z3, t3_send, t3_recv,
    )
    sum_4 = Total(
        NP, S, here_at, remote, gB, out_b, g_sem.at[3], 0, gB.shape[0], None, land_p4, land_z4, t4_send, t4_recv
    )
    up_row, down_row, out_row, gain_row = FF, 2 * FF, 3 * FF, 3 * FF + D

    loads = [
        pltpu.make_async_copy(w.at[:, own_cols], gB.at[pl.ds(i * D, D), own_cols], w_sem.at[i])
        for i, w in enumerate((wq, wk, wv))
    ] + [
        pltpu.make_async_copy(wgT, gA.at[pl.ds(0, FF)], w_sem.at[3]),
        pltpu.make_async_copy(wuT, gA.at[pl.ds(up_row, FF)], w_sem.at[4]),
        pltpu.make_async_copy(wd, gA.at[pl.ds(down_row, FF)], w_sem.at[5]),
        pltpu.make_async_copy(wo, gA.at[pl.ds(out_row, D)], w_sem.at[6]),
    ]
    for load in loads:
        load.start()
    for buffer, used in ((gA, gain_row), (gB, 3 * D)):
        buffer[used:buffer.shape[0], :] = jnp.zeros((buffer.shape[0] - used, D), bf16)
    wo_s = gA.at[pl.ds(out_row, D)]

    barrier = pltpu.get_barrier_semaphore()
    for step in range(1, 2 * S):
        other = lax.rem(c * S + z + step, 2 * S)
        pl.semaphore_signal(
            barrier, inc=1, device_id=(pair + other // S, lax.rem(other, S)), device_id_type=MESH
        )
    for step in range(1, NP):
        pl.semaphore_signal(
            barrier, inc=1, device_id=(2 * lax.rem(pr + step, NP) + c, z), device_id_type=MESH
        )
    pl.semaphore_wait(barrier, 2 * S - 1 + NP - 1)

    seg_copy = remote(seg, seg_other, seg_sem.at[0], seg_sem.at[1], sib, z)
    seg_copy.start()

    def x_rows(index):
        return xs.at[pl.ds(pl.multiple_of(index * T, T), T)]

    def x_copy(l):
        return remote(x.at[l], x_rows(z), x_send.at[l], x_recv.at[z], d, c * G + l)

    own_x = pltpu.make_async_copy(x.at[lz], x_rows(z), loc_sem.at[0])
    own_fwd = remote(x.at[lz], x_rows(z), fwd_send.at[0], x_recv.at[z], sib, z)

    @pl.when(gz == c)
    def _():
        own_x.start()
        own_fwd.start()

    for l in range(G):
        @pl.when(c * G + l != z)
        def _():
            x_copy(l).start()

    for load in loads:
        load.wait()
    for i in range(3):
        wqkvT[i * Dh:(i + 1) * Dh, :] = gB[i * D:(i + 1) * D, own_cols].T
    seg_copy.wait()
    seg_mine = jnp.where(gz == c, seg[...], seg_other[...])
    row = jnp.zeros((1, L), jnp.int32)
    for l in range(G):
        row = jnp.where(lz == l, seg_mine[l:l + 1, :], row)
    ids = row.astype(f32)
    first = jnp.zeros((1, L), f32)
    for doc in range(1, DOCS):
        before = jnp.sum(jnp.where(ids < doc, 1.0, 0.0), axis=1, keepdims=True)
        first = jnp.where(ids >= doc, before, first)
    first_s[...] = jnp.broadcast_to(first, (8, L))
    token = lax.broadcasted_iota(jnp.int32, (1, L), 1).astype(f32)
    place = token - first
    order = lax.broadcasted_iota(jnp.int32, (HD // 2, 1), 0).astype(f32)
    frequency = jnp.exp(order * f32(-2.0 * 9.210340371976184 / HD))
    angle = place * frequency
    cos_s[...] = jnp.cos(angle)
    sin_s[...] = jnp.sin(angle)

    def rms(values):
        inverse = lax.rsqrt(jnp.mean(values * values, axis=-1, keepdims=True) + epsilon)
        return values * inverse, inverse

    def project(start, size):
        rows = pl.ds(start, size)
        plain, _ = rms(xs[rows, :].astype(f32))
        normed = (plain * gain_a[...]).astype(bf16)
        n_s[rows, :] = normed
        lin = dot(wqkvT[...], normed, 1, 1)
        cosine, sine = cos_s[:, rows], sin_s[:, rows]

        def rotated(base):
            parts = []
            for h in range(NH):
                a = lin[base + h * HD:base + h * HD + HD // 2]
                b = lin[base + h * HD + HD // 2:base + (h + 1) * HD]
                parts.append(jnp.concatenate([a * cosine - b * sine, b * cosine + a * sine], axis=0))
            return parts

        query = jnp.concatenate(rotated(0), axis=0).astype(bf16)
        qT[:, rows] = (query.astype(f32) * HD ** -0.5).astype(bf16)
        kT[:, rows] = jnp.concatenate(rotated(Dh), axis=0).astype(bf16)
        vT[:, rows] = lin[2 * Dh:].astype(bf16)

    for step in range(S):
        source = lax.rem(z + step, S)
        arrived = remote(x.at[0], x_rows(source), x_send.at[0], x_recv.at[source], sib, z)
        if step == 0:
            @pl.when(gz == c)
            def _():
                own_x.wait()

            @pl.when(gz != c)
            def _():
                arrived.wait_recv()
        else:
            arrived.wait_recv()

            @pl.when(gz == c)
            def _():
                remote(x_rows(source), x_rows(source), fwd_send.at[step], x_recv.at[source], sib, z).start()

        @pl.loop(0, T // QB)
        def _(i):
            project(pl.multiple_of(source * T + i * QB, QB), QB)

    for l in range(G):
        @pl.when(c * G + l != z)
        def _():
            x_copy(l).wait_send()

    @pl.when(gz == c)
    def _():
        own_fwd.wait_send()
        for step in range(1, S):
            remote(x.at[0], x_rows(z), fwd_send.at[step], x_recv.at[z], sib, z).wait_send()

    to_core = z // G
    slot = lax.rem(z, G)

    def cot_rows(index):
        return cots.at[pl.ds(pl.multiple_of(index * T, T), T)]

    def cot_copy(l):
        return remote(cot.at[l], cot_rows(slot), cot_send.at[l], cot_recv.at[slot], pair + to_core, c * G + l)

    own_cot = pltpu.make_async_copy(cot.at[lz], cot_rows(slot), loc_sem.at[1])
    keeps_own = (gz == c) & (to_core == c)
    for l in range(G):
        here = (c * G + l == z) & (to_core == c)

        @pl.when(jnp.logical_not(here))
        def _():
            cot_copy(l).start()

    @pl.when(keeps_own)
    def _():
        own_cot.start()

    NQ = L // QB

    def place_of(rows, first_row):
        return (lax.broadcasted_iota(jnp.int32, (rows, QB), 0) + first_row).astype(f32)

    def mask_of(tile, qb, kb):
        begin = first_s[0:1, qb * QB:(qb + 1) * QB]
        query_place = (lax.broadcasted_iota(jnp.int32, (1, QB), 1) + qb * QB).astype(f32)
        edge = qb in (0, NQ - 1)
        if edge:
            tile = jnp.where(place_of(QB, kb * QB) >= begin, tile, masked_value)
        elif kb == 0:
            head = jnp.where(place_of(EDGE, 0) >= begin, tile[:EDGE], masked_value)
            tile = jnp.concatenate([head, tile[EDGE:]], axis=0)
        if kb == qb:
            tile = jnp.where(place_of(QB, kb * QB) <= query_place, tile, masked_value)
        return tile

    def mix_copy(h):
        return remote(
            mixT.at[pl.ds(pl.multiple_of(h * HD, HD), HD), pl.ds(pl.multiple_of((1 - c) * half, half), half)],
            mfull.at[pl.ds(pl.multiple_of(c * Dh + h * HD, HD), HD), :],
            mix_send.at[h], mix_recv.at[h], sib, z,
        )

    order = [1] + list(range(NQ - 1, 1, -1)) + [0]

    @pl.loop(0, NH)
    def _(h):
        rows = pl.ds(pl.multiple_of(h * HD, HD), HD)
        tops = {}

        def score(turn):
            qb = order[turn]
            query = qT[rows, qb * QB:(qb + 1) * QB]
            top = None
            for kb in range(qb + 1):
                tile = mask_of(dot(kT[rows, kb * QB:(kb + 1) * QB], query, 0, 0), qb, kb)
                part = jnp.max(tile.reshape(QB // 8, 8, QB), axis=0)
                top = part if top is None else jnp.maximum(top, part)
                s_buf[turn % 2, kb * QB:(kb + 1) * QB, :] = tile
                yield
            tops[turn] = jnp.max(top, axis=0, keepdims=True)

        def weigh(turn):
            qb = order[turn]
            cols = slice(qb * QB, (qb + 1) * QB)
            depth, base = (qb + 1) * QB, strip_offset(qb)
            total = None
            for kb in range(qb + 1):
                expanded = jnp.exp(s_buf[turn % 2, kb * QB:(kb + 1) * QB, :] - tops[turn])
                part = jnp.sum(expanded.reshape(QB // 8, 8, QB), axis=0)
                total = part if total is None else total + part
                p_s[h, base + kb * QB:base + (kb + 1) * QB, :] = expanded.astype(bf16)
                yield
            inverse = 1.0 / jnp.sum(total, axis=0, keepdims=True)
            inv_tot[h, :, cols] = jnp.broadcast_to(inverse, (8, QB))
            low = p_s[h, base:base + depth, :]
            mixT[rows, cols] = (dot(vT[rows, 0:depth], low, 1, 0) * inverse).astype(bf16)

        for _ in score(0):
            pass
        for turn, qb in enumerate(order):
            more = turn + 1 < len(order)
            interleave(
                score(turn + 1) if more else iter(()), order[turn + 1] + 1 if more else 0, weigh(turn), qb + 1
            )
        mix_copy(h).start()
        mfull[pl.ds(pl.multiple_of(c * Dh + h * HD, HD), HD), :] = mixT[
            rows, pl.ds(pl.multiple_of(c * half, half), half)
        ]

    @pl.loop(0, NH)
    def _(h):
        mix_copy(h).wait_send()
        remote(
            mixT.at[0:HD, 0:half], mfull.at[pl.ds(pl.multiple_of((1 - c) * Dh + h * HD, HD), HD), :],
            mix_send.at[h], mix_recv.at[h], sib, z,
        ).wait_recv()

    own_rows = pl.ds(pl.multiple_of(c * Dh, Dh), Dh)

    ff_cuts = [(first_col, min(first_col + 512, FF)) for first_col in range(0, FF, 512)]
    g_gm[...] = jnp.zeros((8, D), f32)
    NB = half // MB
    per = T // MB

    def back_copy(i, src, row, dst, send, recv):
        inside = pl.ds(pl.multiple_of(lax.rem(i, per) * MB, MB), MB)
        return remote(
            src.at[pl.ds(pl.multiple_of(row, MB), MB)], dst.at[lz, inside],
            send.at[i], recv.at[lz * per + lax.rem(i, per)], pair + gz, c * G + i // per,
        )

    def back_local(i, src, row, dst, local):
        inside = pl.ds(pl.multiple_of(lax.rem(i, per) * MB, MB), MB)
        return pltpu.make_async_copy(src.at[pl.ds(pl.multiple_of(row, MB), MB)], dst.at[lz, inside], local.at[lax.rem(i, per)])

    def stays(i):
        return (gz == c) & (c * G + i // per == z)

    def back_start(i, src, row, dst, send, recv, local):
        @pl.when(jnp.logical_not(stays(i)))
        def _():
            back_copy(i, src, row, dst, send, recv).start()

        @pl.when(stays(i))
        def _():
            back_local(i, src, row, dst, local).start()

    def back_wait(src, row, dst, send, recv, local):
        @pl.loop(0, NB)
        def _(i):
            @pl.when(jnp.logical_not(stays(i)))
            def _():
                back_copy(i, src, row + i * MB, dst, send, recv).wait_send()

            @pl.when(stays(i))
            def _():
                back_local(i, src, row + i * MB, dst, local).wait()
        for l in range(G):
            mine = (c * G + l == z) & (gz == c)
            for part in range(per):
                @pl.when(jnp.logical_not(mine))
                def _():
                    remote(
                        src.at[pl.ds(0, MB)], dst.at[l, pl.ds(part * MB, MB)],
                        send.at[0], recv.at[l * per + part], sib, z,
                    ).wait_recv()

    @pl.loop(0, NB)
    def _(i):
        start = pl.multiple_of(i * MB, MB)
        rows = pl.ds(start, MB)
        mine = stays(i)

        @pl.when((lax.rem(i, per) == 0) & jnp.logical_not(mine))
        def _():
            remote(cot.at[0], cot_rows(i // per), cot_send.at[0], cot_recv.at[i // per], sib, z).wait_recv()

        @pl.when((lax.rem(i, per) == 0) & mine)
        def _():
            own_cot.wait()

        base = xs[pl.ds(pl.multiple_of(c * half + start, MB), MB), :].astype(f32)
        middle = base + dot(mfull[:, rows], wo_s[...], 0, 0)
        plain, inverse = rms(middle)
        gain = gain_m[...]
        normed = (plain * gain).astype(bf16)
        nm[rows, :] = normed
        grad = cots[rows, :]
        result = middle
        d_normed = None
        for first_col, last_col in ff_cuts:
            cut = slice(first_col, last_col)
            cut_up = slice(up_row + first_col, up_row + last_col)
            cut_down = slice(down_row + first_col, down_row + last_col)
            gate = dot(normed, gA[cut, :], 1, 1)
            up = dot(normed, gA[cut_up, :], 1, 1)
            sig = 1.0 / (1.0 + jnp.exp(-gate))
            act = gate * sig
            hidden = (act * up).astype(bf16)
            hid[rows, cut] = hidden
            result = result + dot(hidden, gA[cut_down, :], 1, 0)
            d_hidden = dot(grad, gA[cut_down, :], 1, 1)
            d_gate = (d_hidden * up * sig * (1.0 + gate * (1.0 - sig))).astype(bf16)
            d_up = (d_hidden * act).astype(bf16)
            dga[rows, cut] = d_gate
            dup[rows, cut] = d_up
            term = dot(d_gate, gA[cut, :], 1, 0) + dot(d_up, gA[cut_up, :], 1, 0)
            d_normed = term if d_normed is None else d_normed + term
        spare = pl.multiple_of((1 - c) * half + start, MB)
        xs[pl.ds(spare, MB), :] = result.astype(bf16)
        back_start(i, xs, spare, out, out_send, out_recv, loc_sem.at[pl.ds(2, per)])
        scaled = d_normed * gain
        g_gm[...] += fold_rows(d_normed * plain)
        d_middle = grad.astype(f32) + inverse * (scaled - plain * jnp.mean(scaled * plain, axis=-1, keepdims=True))
        d_attn = d_middle.astype(bf16)
        da[rows, :] = d_attn
        dmT[:, rows] = dot(wo_s[...], d_attn, 1, 1).astype(bf16)

    dm_copy = remote(
        dmT.at[pl.ds(pl.multiple_of((1 - c) * Dh, Dh), Dh), :],
        dOT.at[:, pl.ds(pl.multiple_of(c * half, half), half)], dm_send.at[0], dm_recv.at[0], sib, z
    )
    dm_copy.start()

    for l in range(G):
        here = (c * G + l == z) & (to_core == c)

        @pl.when(jnp.logical_not(here))
        def _():
            cot_copy(l).wait_send()

    def ff_grad(target, base, left, right):
        for first_row in range(0, FF, 512):
            last_row = min(first_row + 512, FF)
            grad = dot(left[:, first_row:last_row], right[...], 0, 0)
            target[base + first_row:base + last_row, :] = grad.astype(bf16)

    ff_grad(gA, 0, dga, nm)
    sum_1.start(sum_1.core_scatter())
    ff_grad(gA, up_row, dup, nm)
    ff_grad(gA, down_row, hid, cots)
    sum_2.start(sum_2.core_scatter())
    gA[out_row:out_row + D, :] = dot(mfull[...], da[...], 1, 0).astype(bf16)
    gA[gain_row:gain_row + 16, :] = jnp.concatenate([g_gm[...], jnp.zeros((8, D), f32)], axis=0).astype(bf16)
    sum_3.start(sum_3.core_scatter())
    sum_1.core_add()

    dm_copy.wait()
    dOT[:, pl.ds(pl.multiple_of(c * half, half), half)] = dmT[own_rows, :]
    sum_2.core_add()
    sum_3.core_add()

    parts = (dga, dup, hid)

    def unrotated(values, cosine, sine):
        a, b = values[:HD // 2], values[HD // 2:]
        return jnp.concatenate([a * cosine + b * sine, b * cosine - a * sine], axis=0)

    @pl.loop(0, NH)
    def _(h):
        rows = pl.ds(pl.multiple_of(h * HD, HD), HD)

        def score_back(qb):
            cols = slice(qb * QB, (qb + 1) * QB)
            depth, base = (qb + 1) * QB, strip_offset(qb)
            grad_wide = dOT[rows, cols].astype(f32) * inv_tot[h, 0:1, cols]
            delta = jnp.sum(grad_wide * mixT[rows, cols].astype(f32), axis=0, keepdims=True)
            grad = grad_wide.astype(bf16)
            add_v = dot(grad, p_s[h, base:base + depth, :], 1, 1)
            if qb == NQ - 1:
                dacc_v[:, 0:depth] = add_v
            else:
                dacc_v[:, 0:depth] += add_v
            yield
            for kb in range(qb + 1):
                tile = slice(base + kb * QB, base + (kb + 1) * QB)
                d_probs = dot(vT[rows, kb * QB:(kb + 1) * QB], grad, 0, 0)
                p_s[h, tile, :] = (p_s[h, tile, :].astype(f32) * (d_probs - delta)).astype(bf16)
                yield

        def spread_back(qb):
            cols = slice(qb * QB, (qb + 1) * QB)
            depth, base = (qb + 1) * QB, strip_offset(qb)
            d_scores = p_s[h, base:base + depth, :]
            add_k = dot(qT[rows, cols], d_scores, 1, 1)
            if qb == NQ - 1:
                dacc_k[:, 0:depth] = add_k
            else:
                dacc_k[:, 0:depth] += add_k
            yield
            d_query = dot(kT[rows, 0:depth], d_scores, 1, 0) * HD ** -0.5
            side, lane = divmod(qb * QB, half)
            parts[0][pl.ds(pl.multiple_of(side * Dh + h * HD, HD), HD), lane:lane + QB] = unrotated(
                d_query.astype(bf16).astype(f32), cos_s[:, cols], sin_s[:, cols]
            ).astype(bf16)
            yield

        for _ in score_back(NQ - 1):
            pass
        for qb in reversed(range(NQ)):
            interleave(score_back(qb - 1) if qb else iter(()), qb + 1 if qb else 0, spread_back(qb), 2)
        for side in range(2):
            cols = slice(side * half, (side + 1) * half)
            place_rows = pl.ds(pl.multiple_of(side * Dh + h * HD, HD), HD)
            parts[1][place_rows, 0:half] = unrotated(
                dacc_k[:, cols].astype(bf16).astype(f32), cos_s[:, cols], sin_s[:, cols]
            ).astype(bf16)
            parts[2][place_rows, 0:half] = dacc_v[:, cols].astype(bf16)
        pl.when(h == 1)(sum_1.pair_add)

    sum_2.pair_add()
    sum_1.z_add()

    def back_norm(side, start):
        side_rows = pl.ds(pl.multiple_of(side * Dh, Dh), Dh)
        total = None
        for i in range(3):
            term = dot(parts[i][side_rows, pl.ds(start, MB)], wqkvT[i * Dh:(i + 1) * Dh, :], 0, 0)
            total = term if total is None else total + term
        return total

    @pl.loop(0, half // MB)
    def _(i):
        start = pl.multiple_of(i * MB, MB)
        nm[pl.ds(start, MB), :] = back_norm(1 - c, start).astype(bf16)

    dn_in = cots
    dn_copy = remote(nm, dn_in, dn_send.at[0], dn_recv.at[0], sib, z)
    dn_copy.start()

    for i in range(3):
        grad = dot(parts[i][0:Dh, 0:half], n_s[0:half, :], 1, 0)
        grad = grad + dot(parts[i][Dh:2 * Dh, 0:half], n_s[half:L, :], 1, 0)
        gB[i * D:(i + 1) * D, own_cols] = grad.T.astype(bf16)
    back_wait(xs, (1 - c) * half, out, out_send, out_recv, loc_sem.at[pl.ds(2, per)])
    dn_copy.wait()

    g_ga[...] = jnp.zeros((8, D), f32)

    @pl.loop(0, NB)
    def _(i):
        start = pl.multiple_of(i * MB, MB)
        rows = pl.ds(start, MB)
        own = pl.ds(pl.multiple_of(c * half + start, MB), MB)
        d_normed = back_norm(c, start) + dn_in[rows, :].astype(f32)
        plain, inverse = rms(xs[own, :].astype(f32))
        scaled = d_normed * gain_a[...]
        g_ga[...] += fold_rows(d_normed * plain)
        d_start = inverse * (scaled - plain * jnp.mean(scaled * plain, axis=-1, keepdims=True))
        nm[rows, :] = (da[rows, :].astype(f32) + d_start).astype(bf16)
        back_start(i, nm, start, gin, gin_send, gin_recv, loc_sem.at[pl.ds(2 + per, per)])

    gB[3 * D:3 * D + 16, own_cols] = jnp.concatenate([g_ga[:, :Dh], g_ga[:, Dh:]], axis=0).astype(bf16)
    sum_4.start(sum_4.pair_scatter())
    sum_1.z_done()
    sum_3.pair_add()
    sum_2.z_add()
    sum_1.pair_done()
    sum_2.z_done()
    sum_3.z_add()
    sum_4.pair_add()
    sum_3.z_done()
    sum_1.core_done()
    sum_2.pair_done()
    sum_4.z_add()
    sum_3.pair_done()
    sum_4.z_done()
    sum_2.core_done()
    sum_4.pair_done()
    sum_3.core_done()
    back_wait(nm, 0, gin, gin_send, gin_recv, loc_sem.at[pl.ds(2 + per, per)])
    sum_4.core_done()


def on_device(
    G, S, NP,
    inputs, segment_ids, cotangent, norm_attn, norm_mlp, w_query, w_key, w_value, w_out, w_gate, w_up, w_down,
):
    _, T, D = inputs.shape
    FF = w_gate.shape[1]
    L = T * S
    half, Dh = L // 2, D // 2
    NH = Dh // HD
    anywhere = pl.BlockSpec(memory_space=pl.ANY)
    vmem = pl.BlockSpec(memory_space=pltpu.VMEM)
    dma = pltpu.SemaphoreType.DMA

    def buf(*shape, dtype=bf16):
        return pltpu.VMEM(shape, dtype)

    strips = strip_offset(L // QB)
    shards = NP * S
    RA, RB = padded(3 * FF + D + 16, shards), padded(3 * D + 16, shards)

    def lands(rows, core):
        kept = [buf(rows, Dh)] if core else []
        return kept + [buf(NP - 1, rows // NP, Dh), buf(S - 1, rows // shards, Dh)]

    steps = 2 + 2 * (NP - 1) + 2 * (S - 1)
    NB, per = half // MB, T // MB
    out, gin, out_a, out_b = pl.pallas_call(
        functools.partial(block_kernel, G, S, NP, T, L, D, FF),
        out_shape=[
            jax.ShapeDtypeStruct((G, T, D), bf16),
            jax.ShapeDtypeStruct((G, T, D), bf16),
            jax.ShapeDtypeStruct((RA, D), bf16),
            jax.ShapeDtypeStruct((RB, D), bf16),
        ],
        in_specs=[anywhere, vmem, anywhere, vmem, vmem] + [anywhere] * 7,
        out_specs=[anywhere] * 4,
        scratch_shapes=[
            buf(L, D), buf(half, D), buf(G, L, dtype=jnp.int32), buf(8, L, dtype=f32),
            buf(HD // 2, L, dtype=f32), buf(HD // 2, L, dtype=f32),
            buf(L, D), buf(3 * Dh, D), buf(RA, D), buf(RB, D),
            buf(Dh, L), buf(Dh, L), buf(Dh, L),
            buf(NH, strips, QB), buf(2, L, QB, dtype=f32), buf(NH, 8, L, dtype=f32), buf(Dh, L), buf(D, half),
            buf(half, D), buf(half, FF), buf(half, FF), buf(half, FF),
            buf(half, D), buf(D, half),
            buf(Dh, L), buf(HD, L, dtype=f32), buf(HD, L, dtype=f32),
            buf(8, D, dtype=f32), buf(8, D, dtype=f32),
            *(land for rows in split_rows(RA, FF, shards) for land in lands(rows, True)), *lands(RB, False),
            dma((7,)), dma((2 + 2 * per,)), dma((2,)), dma((G,)), dma((S,)), dma((S,)), dma((G,)), dma((G,)),
            dma((NH,)), dma((NH,)), dma((NB,)), dma((G * per,)), dma((1,)), dma((1,)), dma((1,)), dma((1,)),
            dma((NB,)), dma((G * per,)), dma((4,)),
            *([dma((steps,))] * 8),
        ],
        compiler_params=pltpu.CompilerParams(
            collective_id=0, has_side_effects=True, vmem_limit_bytes=63 * 2**20
        ),
    )(
        inputs, segment_ids, cotangent, norm_attn.reshape(1, D), norm_mlp.reshape(1, D),
        w_query, w_key, w_value, w_out, w_gate.T, w_up.T, w_down,
    )

    last_a, last_b = 3 * FF + D, 3 * D
    gain_attn = jnp.sum(out_b[last_b:last_b + 16].astype(f32).reshape(2, 8, 2, Dh), axis=(1, 2)).reshape(D)
    gain_mlp = jnp.sum(out_a[last_a:last_a + 8].astype(f32), axis=0)
    return (
        out, gin.astype(f32), gain_attn, gain_mlp,
        out_b[:D].astype(f32), out_b[D:2 * D].astype(f32), out_b[2 * D:3 * D].astype(f32),
        out_a[3 * FF:last_a].astype(f32), out_a[:FF].astype(f32).T, out_a[FF:2 * FF].astype(f32).T,
        out_a[2 * FF:3 * FF].astype(f32),
    )


def solution(mesh):
    S = mesh.shape["seq"]
    NP = mesh.shape["dp"] // 2
    rows = P("dp", "seq", None)
    return jax.shard_map(
        functools.partial(on_device, S // 2, S, NP),
        mesh=mesh,
        in_specs=(rows, P("dp", None), rows) + (P(),) * 9,
        out_specs=(rows, rows) + (P(),) * 9,
        check_vma=False,
    )
```

```python
import functools

import jax
import jax.numpy as jnp
from jax import lax
from jax.experimental import pallas as pl
from jax.experimental.pallas import tpu as pltpu
from jax.sharding import PartitionSpec as P

HD = 64
DOCS = 7
epsilon = 1e-05
theta_base = 10000.0
masked_value = -1e30
MESH = pl.DeviceIdType.MESH
f32 = jnp.float32
bf16 = jnp.bfloat16
QB = 256
MB = 256
SCHEDULE = (
    4, 3, 1, 0, 2, 5, 3, 1, 2, 4, 6, 3, 5, 4, 2, 0, 1, 7, 3, 2, 8, 5,
    0, 9, 0, 1, 1, 2, 3, 2, 3, 5, 5,
)
EDGE = 128


def dot(left, right, left_dim, right_dim):
    return lax.dot_general(
        left, right, (((left_dim,), (right_dim,)), ((), ())), preferred_element_type=f32
    )


def strip_offset(block):
    return QB * block * (block + 1) // 2


def padded(rows, shards):
    unit = 16 * shards
    return (rows + unit - 1) // unit * unit


class Axis:
    def __init__(self, size, index, device):
        self.size, self.index, self.device = size, index, device

    def others(self):
        return [lax.rem(self.index + k, self.size) for k in range(1, self.size)]


def lands(rows, sizes, core, width):
    shapes = [(rows, width)] if core else []
    for size in sizes:
        rows //= size
        shapes.append((size - 1, rows, width))
    return shapes


def copies_of(sizes):
    return 2 + 2 * sum(size - 1 for size in sizes)


class Total:
    def __init__(self, remote, core, axes, own, other, buf, result, local, base, count, land, send, recv):
        self.remote, self.core, self.axes, self.own, self.other = remote, core, axes, own, other
        self.buf, self.result, self.local = buf, result, local
        self.base, self.count = base, count
        self.send, self.recv = send, recv
        sizes = [axis.size for axis in axes]
        self.with_core = len(land) > len(sizes)
        self.land = list(land)
        self.starts, self.counts, self.first_sem = [base], [count], [2]
        for axis in axes:
            self.counts.append(self.counts[-1] // axis.size)
            self.starts.append(self.starts[-1] + axis.index * self.counts[-1])
            self.first_sem.append(self.first_sem[-1] + 2 * (axis.size - 1))
        self.stages = [("core", 0)] if self.with_core else []
        self.stages += [("scatter", k) for k in range(len(axes))]
        self.stages += [("gather", k) for k in reversed(range(len(axes)))]
        self.stages.append(("back", 0))
        self.at = 0

    def rows(self, start, count):
        return pl.ds(pl.multiple_of(start, 16), count)

    def copies(self, stage):
        kind, k = stage
        if kind == "core":
            src = self.buf.at[pl.ds(self.base, self.count), self.other]
            return [self.remote(src, self.land[0], self.send.at[0], self.recv.at[0], *self.core)]
        if kind == "back":
            half = self.result.at[pl.ds(self.base, self.count), self.own]
            return [self.remote(half, half, self.send.at[1], self.recv.at[1], *self.core)]
        axis, count = self.axes[k], self.counts[k + 1]
        land = self.land[k + self.with_core]
        made = []
        for slot, to in enumerate(axis.others()):
            if kind == "scatter":
                src = self.buf.at[self.rows(self.starts[k] + to * count, count), self.own]
                dst, sem = land.at[slot], self.first_sem[k] + slot
            else:
                rows = self.rows(self.starts[k + 1], count)
                source = self.buf if k == len(self.axes) - 1 else self.result
                src, dst = source.at[rows, self.own], self.result.at[rows, self.own]
                sem = self.first_sem[k] + axis.size - 1 + slot
            made.append(self.remote(src, dst, self.send.at[sem], self.recv.at[sem], *axis.device(to)))
        if kind == "gather" and k == len(self.axes) - 1:
            rows = self.rows(self.starts[k + 1], count)
            made.append(pltpu.make_async_copy(self.buf.at[rows, self.own], self.result.at[rows, self.own], self.local))
        return made

    def add(self, start, count, land):
        chunk = self.counts[-1]

        @pl.loop(0, count // chunk)
        def _(i):
            rows = self.rows(start + i * chunk, chunk)
            total = self.buf[rows, self.own].astype(f32)
            for piece in land:
                total = total + piece[self.rows(i * chunk, chunk), :].astype(f32)
            self.buf[rows, self.own] = total.astype(bf16)

    def begin(self):
        for copy in self.copies(self.stages[self.at]):
            copy.start()

    def advance(self):
        kind, k = stage = self.stages[self.at]
        for copy in self.copies(stage):
            copy.wait()
        if kind == "core":
            self.add(self.base, self.count, [self.land[0]])
        elif kind == "scatter":
            land = self.land[k + self.with_core]
            self.add(self.starts[k + 1], self.counts[k + 1], [land.at[slot] for slot in range(self.axes[k].size - 1)])
        self.at += 1
        if self.at < len(self.stages):
            self.begin()


def fold_rows(values):
    rows, width = values.shape
    return jnp.sum(values.reshape(rows // 8, 8, width), axis=0)


def split_rows(rows, first, second, shards):
    unit = 16 * shards
    edges = [0, first // unit * unit, second // unit * unit]
    edges += [(edges[2] + rows + unit) // 2 // unit * unit, rows]
    return [(start, end - start) for start, end in zip(edges, edges[1:])]


def axis_sizes(NP, S):
    fast = 2 if NP % 2 == 0 else 1
    return [fast, NP // fast, 2, S // 2], [NP // fast, fast, 2, S // 2], [NP, S]


def interleave(main, count_main, side, count_side):
    steps = max(count_main, count_side)
    done_main = done_side = 0
    for step in range(1, steps + 1):
        while done_main < step * count_main / steps:
            next(main, None)
            done_main += 1
        while done_side < step * count_side / steps:
            next(side, None)
            done_side += 1
    for _ in main:
        pass
    for _ in side:
        pass


def block_kernel(
    G, S, NP, T, L, D, FF,
    x, seg, cot, gain_a, gain_m, wq, wk, wv, wo, wgT, wuT, wd,
    out, gin, out_a, out_b,
    xs, cots, seg_other, first_s, cos_s, sin_s, n_s, wqkvT, gA, gB,
    qT, kT, vT, p_s, s_buf, inv_tot, mixT, mfull, nm, hid, dga, dup, da, dmT,
    dOT, dacc_k, dacc_v, g_ga, g_gm,
    w_sem, loc_sem, seg_sem, x_send, x_recv, fwd_send, cot_send, cot_recv, mix_send, mix_recv,
    out_send, out_recv, dm_send, dm_recv, dn_send, dn_recv, gin_send, gin_recv, g_sem,
    *rest,
):
    d = lax.axis_index("dp")
    z = lax.axis_index("seq")
    c = lax.rem(d, 2)
    pair = d - c
    sib = pair + 1 - c
    gz = z // G
    lz = lax.rem(z, G)
    half = L // 2
    Dh = D // 2
    NH = Dh // HD

    def remote(src, dst, send, recv, dp, seq):
        return pltpu.make_async_remote_copy(
            src_ref=src, dst_ref=dst, send_sem=send, recv_sem=recv,
            device_id=(dp, seq), device_id_type=MESH,
        )

    own_cols = pl.ds(pl.multiple_of(c * Dh, Dh), Dh)
    other_cols = pl.ds(pl.multiple_of((1 - c) * Dh, Dh), Dh)
    pr = d // 2
    fast = 2 if NP % 2 == 0 else 1
    row_at, col_at = pr // fast, lax.rem(pr, fast)
    low, high = lax.rem(z, 2), z // 2
    axis_x = Axis(fast, col_at, lambda j: (2 * (row_at * fast + j) + c, z))
    axis_y = Axis(NP // fast, row_at, lambda j: (2 * (j * fast + col_at) + c, z))
    axis_near = Axis(2, low, lambda j: (d, high * 2 + j))
    axis_far = Axis(S // 2, high, lambda j: (d, j * 2 + low))
    rest = list(rest)

    def take(count):
        taken = rest[:count]
        del rest[:count]
        return taken

    axis_pairs = Axis(NP, pr, lambda j: (2 * j + c, z))
    axis_z = Axis(S, z, lambda j: (d, j))
    sums = []
    for k, (base, count) in enumerate(split_rows(gA.shape[0], FF, 2 * FF, NP * S)):
        axes = ([axis_x, axis_y] if k % 2 == 0 else [axis_y, axis_x]) + [axis_near, axis_far]
        land = take(len(axes) + 1)
        send, recv = take(2)
        sums.append(Total(
            remote, (sib, z), axes, own_cols, other_cols, gA, out_a, g_sem.at[k], base, count, land, send, recv,
        ))
    quarter = Dh // 2
    side_cols = [pl.ds(pl.multiple_of(c * Dh + k * quarter, quarter), quarter) for k in range(2)]
    for k in range(2):
        land = take(2)
        send, recv = take(2)
        sums.append(Total(
            remote, (sib, z), [axis_pairs, axis_z], side_cols[k], None, gB, out_b, g_sem.at[4 + k], 0, gB.shape[0],
            land, send, recv,
        ))
    a1, a2, a3, a4, b1, b2 = sums

    def advance(*several):
        for each in several:
            each.advance()

    up_row, down_row, out_row, gain_row = FF, 2 * FF, 3 * FF, 3 * FF + D

    loads = [
        pltpu.make_async_copy(w.at[:, own_cols], gB.at[pl.ds(i * D, D), own_cols], w_sem.at[i])
        for i, w in enumerate((wq, wk, wv))
    ] + [
        pltpu.make_async_copy(wgT, gA.at[pl.ds(0, FF)], w_sem.at[3]),
        pltpu.make_async_copy(wuT, gA.at[pl.ds(up_row, FF)], w_sem.at[4]),
        pltpu.make_async_copy(wd, gA.at[pl.ds(down_row, FF)], w_sem.at[5]),
        pltpu.make_async_copy(wo, gA.at[pl.ds(out_row, D)], w_sem.at[6]),
    ]
    for load in loads:
        load.start()
    for buffer, used in ((gA, gain_row), (gB, 3 * D)):
        buffer[used:buffer.shape[0], :] = jnp.zeros((buffer.shape[0] - used, D), bf16)
    wo_s = gA.at[pl.ds(out_row, D)]

    barrier = pltpu.get_barrier_semaphore()
    for step in range(1, 2 * S):
        other = lax.rem(c * S + z + step, 2 * S)
        pl.semaphore_signal(
            barrier, inc=1, device_id=(pair + other // S, lax.rem(other, S)), device_id_type=MESH
        )
    for step in range(1, NP):
        pl.semaphore_signal(
            barrier, inc=1, device_id=(2 * lax.rem(pr + step, NP) + c, z), device_id_type=MESH
        )
    pl.semaphore_wait(barrier, 2 * S - 1 + NP - 1)

    seg_copy = remote(seg, seg_other, seg_sem.at[0], seg_sem.at[1], sib, z)
    seg_copy.start()

    def x_rows(index):
        return xs.at[pl.ds(pl.multiple_of(index * T, T), T)]

    def x_copy(l):
        return remote(x.at[l], x_rows(z), x_send.at[l], x_recv.at[z], d, c * G + l)

    own_x = pltpu.make_async_copy(x.at[lz], x_rows(z), loc_sem.at[0])
    own_fwd = remote(x.at[lz], x_rows(z), fwd_send.at[0], x_recv.at[z], sib, z)

    @pl.when(gz == c)
    def _():
        own_x.start()
        own_fwd.start()

    for l in range(G):
        @pl.when(c * G + l != z)
        def _():
            x_copy(l).start()

    for load in loads:
        load.wait()
    for i in range(3):
        wqkvT[i * Dh:(i + 1) * Dh, :] = gB[i * D:(i + 1) * D, own_cols].T
    seg_copy.wait()
    seg_mine = jnp.where(gz == c, seg[...], seg_other[...])
    row = jnp.zeros((1, L), jnp.int32)
    for l in range(G):
        row = jnp.where(lz == l, seg_mine[l:l + 1, :], row)
    ids = row.astype(f32)
    first = jnp.zeros((1, L), f32)
    for doc in range(1, DOCS):
        before = jnp.sum(jnp.where(ids < doc, 1.0, 0.0), axis=1, keepdims=True)
        first = jnp.where(ids >= doc, before, first)
    first_s[...] = jnp.broadcast_to(first, (8, L))
    token = lax.broadcasted_iota(jnp.int32, (1, L), 1).astype(f32)
    place = token - first
    order = lax.broadcasted_iota(jnp.int32, (HD // 2, 1), 0).astype(f32)
    frequency = jnp.exp(order * f32(-2.0 * 9.210340371976184 / HD))
    angle = place * frequency
    cos_s[...] = jnp.cos(angle)
    sin_s[...] = jnp.sin(angle)

    def rms(values):
        inverse = lax.rsqrt(jnp.mean(values * values, axis=-1, keepdims=True) + epsilon)
        return values * inverse, inverse

    def project(start, size):
        rows = pl.ds(start, size)
        plain, _ = rms(xs[rows, :].astype(f32))
        normed = (plain * gain_a[...]).astype(bf16)
        n_s[rows, :] = normed
        lin = dot(wqkvT[...], normed, 1, 1)
        cosine, sine = cos_s[:, rows], sin_s[:, rows]

        def rotated(base):
            parts = []
            for h in range(NH):
                a = lin[base + h * HD:base + h * HD + HD // 2]
                b = lin[base + h * HD + HD // 2:base + (h + 1) * HD]
                parts.append(jnp.concatenate([a * cosine - b * sine, b * cosine + a * sine], axis=0))
            return parts

        query = jnp.concatenate(rotated(0), axis=0).astype(bf16)
        qT[:, rows] = (query.astype(f32) * HD ** -0.5).astype(bf16)
        kT[:, rows] = jnp.concatenate(rotated(Dh), axis=0).astype(bf16)
        vT[:, rows] = lin[2 * Dh:].astype(bf16)

    for step in range(S):
        source = lax.rem(z + step, S)
        arrived = remote(x.at[0], x_rows(source), x_send.at[0], x_recv.at[source], sib, z)
        if step == 0:
            @pl.when(gz == c)
            def _():
                own_x.wait()

            @pl.when(gz != c)
            def _():
                arrived.wait_recv()
        else:
            arrived.wait_recv()

            @pl.when(gz == c)
            def _():
                remote(x_rows(source), x_rows(source), fwd_send.at[step], x_recv.at[source], sib, z).start()

        @pl.loop(0, T // QB)
        def _(i):
            project(pl.multiple_of(source * T + i * QB, QB), QB)

    for l in range(G):
        @pl.when(c * G + l != z)
        def _():
            x_copy(l).wait_send()

    @pl.when(gz == c)
    def _():
        own_fwd.wait_send()
        for step in range(1, S):
            remote(x.at[0], x_rows(z), fwd_send.at[step], x_recv.at[z], sib, z).wait_send()

    to_core = z // G
    slot = lax.rem(z, G)

    def cot_rows(index):
        return cots.at[pl.ds(pl.multiple_of(index * T, T), T)]

    def cot_copy(l):
        return remote(cot.at[l], cot_rows(slot), cot_send.at[l], cot_recv.at[slot], pair + to_core, c * G + l)

    own_cot = pltpu.make_async_copy(cot.at[lz], cot_rows(slot), loc_sem.at[1])
    keeps_own = (gz == c) & (to_core == c)
    for l in range(G):
        here = (c * G + l == z) & (to_core == c)

        @pl.when(jnp.logical_not(here))
        def _():
            cot_copy(l).start()

    @pl.when(keeps_own)
    def _():
        own_cot.start()

    NQ = L // QB

    def place_of(rows, first_row):
        return (lax.broadcasted_iota(jnp.int32, (rows, QB), 0) + first_row).astype(f32)

    def mask_of(tile, qb, kb):
        begin = first_s[0:1, qb * QB:(qb + 1) * QB]
        query_place = (lax.broadcasted_iota(jnp.int32, (1, QB), 1) + qb * QB).astype(f32)
        edge = qb in (0, NQ - 1)
        if edge:
            tile = jnp.where(place_of(QB, kb * QB) >= begin, tile, masked_value)
        elif kb == 0:
            head = jnp.where(place_of(EDGE, 0) >= begin, tile[:EDGE], masked_value)
            tile = jnp.concatenate([head, tile[EDGE:]], axis=0)
        if kb == qb:
            tile = jnp.where(place_of(QB, kb * QB) <= query_place, tile, masked_value)
        return tile

    def mix_copy(h):
        return remote(
            mixT.at[pl.ds(pl.multiple_of(h * HD, HD), HD), pl.ds(pl.multiple_of((1 - c) * half, half), half)],
            mfull.at[pl.ds(pl.multiple_of(c * Dh + h * HD, HD), HD), :],
            mix_send.at[h], mix_recv.at[h], sib, z,
        )

    order = [1] + list(range(NQ - 1, 1, -1)) + [0]

    @pl.loop(0, NH)
    def _(h):
        rows = pl.ds(pl.multiple_of(h * HD, HD), HD)
        tops = {}

        def score(turn):
            qb = order[turn]
            query = qT[rows, qb * QB:(qb + 1) * QB]
            top = None
            for kb in range(qb + 1):
                tile = mask_of(dot(kT[rows, kb * QB:(kb + 1) * QB], query, 0, 0), qb, kb)
                part = jnp.max(tile.reshape(QB // 8, 8, QB), axis=0)
                top = part if top is None else jnp.maximum(top, part)
                s_buf[turn % 2, kb * QB:(kb + 1) * QB, :] = tile
                yield
            tops[turn] = jnp.max(top, axis=0, keepdims=True)

        def weigh(turn):
            qb = order[turn]
            cols = slice(qb * QB, (qb + 1) * QB)
            depth, base = (qb + 1) * QB, strip_offset(qb)
            total = None
            for kb in range(qb + 1):
                expanded = jnp.exp(s_buf[turn % 2, kb * QB:(kb + 1) * QB, :] - tops[turn])
                part = jnp.sum(expanded.reshape(QB // 8, 8, QB), axis=0)
                total = part if total is None else total + part
                p_s[h, base + kb * QB:base + (kb + 1) * QB, :] = expanded.astype(bf16)
                yield
            inverse = 1.0 / jnp.sum(total, axis=0, keepdims=True)
            inv_tot[h, :, cols] = jnp.broadcast_to(inverse, (8, QB))
            low = p_s[h, base:base + depth, :]
            mixT[rows, cols] = (dot(vT[rows, 0:depth], low, 1, 0) * inverse).astype(bf16)

        for _ in score(0):
            pass
        for turn, qb in enumerate(order):
            more = turn + 1 < len(order)
            interleave(
                score(turn + 1) if more else iter(()), order[turn + 1] + 1 if more else 0, weigh(turn), qb + 1
            )
        mix_copy(h).start()
        mfull[pl.ds(pl.multiple_of(c * Dh + h * HD, HD), HD), :] = mixT[
            rows, pl.ds(pl.multiple_of(c * half, half), half)
        ]

    @pl.loop(0, NH)
    def _(h):
        mix_copy(h).wait_send()
        remote(
            mixT.at[0:HD, 0:half], mfull.at[pl.ds(pl.multiple_of((1 - c) * Dh + h * HD, HD), HD), :],
            mix_send.at[h], mix_recv.at[h], sib, z,
        ).wait_recv()

    own_rows = pl.ds(pl.multiple_of(c * Dh, Dh), Dh)

    ff_cuts = [(first_col, min(first_col + 512, FF)) for first_col in range(0, FF, 512)]
    g_gm[...] = jnp.zeros((8, D), f32)
    NB = half // MB
    per = T // MB

    def back_copy(i, src, row, dst, send, recv):
        inside = pl.ds(pl.multiple_of(lax.rem(i, per) * MB, MB), MB)
        return remote(
            src.at[pl.ds(pl.multiple_of(row, MB), MB)], dst.at[lz, inside],
            send.at[i], recv.at[lz * per + lax.rem(i, per)], pair + gz, c * G + i // per,
        )

    def back_local(i, src, row, dst, local):
        inside = pl.ds(pl.multiple_of(lax.rem(i, per) * MB, MB), MB)
        return pltpu.make_async_copy(src.at[pl.ds(pl.multiple_of(row, MB), MB)], dst.at[lz, inside], local.at[lax.rem(i, per)])

    def stays(i):
        return (gz == c) & (c * G + i // per == z)

    def back_start(i, src, row, dst, send, recv, local):
        @pl.when(jnp.logical_not(stays(i)))
        def _():
            back_copy(i, src, row, dst, send, recv).start()

        @pl.when(stays(i))
        def _():
            back_local(i, src, row, dst, local).start()

    def back_wait(src, row, dst, send, recv, local):
        @pl.loop(0, NB)
        def _(i):
            @pl.when(jnp.logical_not(stays(i)))
            def _():
                back_copy(i, src, row + i * MB, dst, send, recv).wait_send()

            @pl.when(stays(i))
            def _():
                back_local(i, src, row + i * MB, dst, local).wait()
        for l in range(G):
            mine = (c * G + l == z) & (gz == c)
            for part in range(per):
                @pl.when(jnp.logical_not(mine))
                def _():
                    remote(
                        src.at[pl.ds(0, MB)], dst.at[l, pl.ds(part * MB, MB)],
                        send.at[0], recv.at[l * per + part], sib, z,
                    ).wait_recv()

    @pl.loop(0, NB)
    def _(i):
        start = pl.multiple_of(i * MB, MB)
        rows = pl.ds(start, MB)
        mine = stays(i)

        @pl.when((lax.rem(i, per) == 0) & jnp.logical_not(mine))
        def _():
            remote(cot.at[0], cot_rows(i // per), cot_send.at[0], cot_recv.at[i // per], sib, z).wait_recv()

        @pl.when((lax.rem(i, per) == 0) & mine)
        def _():
            own_cot.wait()

        base = xs[pl.ds(pl.multiple_of(c * half + start, MB), MB), :].astype(f32)
        middle = base + dot(mfull[:, rows], wo_s[...], 0, 0)
        plain, inverse = rms(middle)
        gain = gain_m[...]
        normed = (plain * gain).astype(bf16)
        nm[rows, :] = normed
        grad = cots[rows, :]
        result = middle
        d_normed = None
        for first_col, last_col in ff_cuts:
            cut = slice(first_col, last_col)
            cut_up = slice(up_row + first_col, up_row + last_col)
            cut_down = slice(down_row + first_col, down_row + last_col)
            gate = dot(normed, gA[cut, :], 1, 1)
            up = dot(normed, gA[cut_up, :], 1, 1)
            sig = 1.0 / (1.0 + jnp.exp(-gate))
            act = gate * sig
            hidden = (act * up).astype(bf16)
            hid[rows, cut] = hidden
            result = result + dot(hidden, gA[cut_down, :], 1, 0)
            d_hidden = dot(grad, gA[cut_down, :], 1, 1)
            d_gate = (d_hidden * up * sig * (1.0 + gate * (1.0 - sig))).astype(bf16)
            d_up = (d_hidden * act).astype(bf16)
            dga[rows, cut] = d_gate
            dup[rows, cut] = d_up
            term = dot(d_gate, gA[cut, :], 1, 0) + dot(d_up, gA[cut_up, :], 1, 0)
            d_normed = term if d_normed is None else d_normed + term
        spare = pl.multiple_of((1 - c) * half + start, MB)
        xs[pl.ds(spare, MB), :] = result.astype(bf16)
        back_start(i, xs, spare, out, out_send, out_recv, loc_sem.at[pl.ds(2, per)])
        scaled = d_normed * gain
        g_gm[...] += fold_rows(d_normed * plain)
        d_middle = grad.astype(f32) + inverse * (scaled - plain * jnp.mean(scaled * plain, axis=-1, keepdims=True))
        d_attn = d_middle.astype(bf16)
        da[rows, :] = d_attn
        dmT[:, rows] = dot(wo_s[...], d_attn, 1, 1).astype(bf16)

    dm_copy = remote(
        dmT.at[pl.ds(pl.multiple_of((1 - c) * Dh, Dh), Dh), :],
        dOT.at[:, pl.ds(pl.multiple_of(c * half, half), half)], dm_send.at[0], dm_recv.at[0], sib, z
    )
    dm_copy.start()

    for l in range(G):
        here = (c * G + l == z) & (to_core == c)

        @pl.when(jnp.logical_not(here))
        def _():
            cot_copy(l).wait_send()

    def ff_grad(target, base, left, right):
        for first_row in range(0, FF, 512):
            last_row = min(first_row + 512, FF)
            grad = dot(left[:, first_row:last_row], right[...], 0, 0)
            target[base + first_row:base + last_row, :] = grad.astype(bf16)

    ff_grad(gA, 0, dga, nm)
    a1.begin()
    ff_grad(gA, up_row, dup, nm)
    a2.begin()
    ff_grad(gA, down_row, hid, cots)
    a3.begin()
    advance(a1)
    gA[out_row:out_row + D, :] = dot(mfull[...], da[...], 1, 0).astype(bf16)
    gA[gain_row:gain_row + 16, :] = jnp.concatenate([g_gm[...], jnp.zeros((8, D), f32)], axis=0).astype(bf16)
    a4.begin()
    advance(a2, a3)

    dm_copy.wait()
    dOT[:, pl.ds(pl.multiple_of(c * half, half), half)] = dmT[own_rows, :]
    parts = (dga, dup, hid)

    def lin_grads(side):
        rows = slice(side * quarter, (side + 1) * quarter)
        late = slice(Dh + side * quarter, Dh + (side + 1) * quarter)
        for i in range(3):
            grad = dot(parts[i][rows, 0:half], n_s[0:half, :], 1, 0)
            grad = grad + dot(parts[i][late, 0:half], n_s[half:L, :], 1, 0)
            gB[i * D:(i + 1) * D, side_cols[side]] = grad.T.astype(bf16)

    def unrotated(values, cosine, sine):
        a, b = values[:HD // 2], values[HD // 2:]
        return jnp.concatenate([a * cosine + b * sine, b * cosine - a * sine], axis=0)

    @pl.loop(0, NH)
    def _(h):
        rows = pl.ds(pl.multiple_of(h * HD, HD), HD)

        def score_back(qb):
            cols = slice(qb * QB, (qb + 1) * QB)
            depth, base = (qb + 1) * QB, strip_offset(qb)
            grad_wide = dOT[rows, cols].astype(f32) * inv_tot[h, 0:1, cols]
            delta = jnp.sum(grad_wide * mixT[rows, cols].astype(f32), axis=0, keepdims=True)
            grad = grad_wide.astype(bf16)
            add_v = dot(grad, p_s[h, base:base + depth, :], 1, 1)
            if qb == NQ - 1:
                dacc_v[:, 0:depth] = add_v
            else:
                dacc_v[:, 0:depth] += add_v
            yield
            for kb in range(qb + 1):
                tile = slice(base + kb * QB, base + (kb + 1) * QB)
                d_probs = dot(vT[rows, kb * QB:(kb + 1) * QB], grad, 0, 0)
                p_s[h, tile, :] = (p_s[h, tile, :].astype(f32) * (d_probs - delta)).astype(bf16)
                yield

        def spread_back(qb):
            cols = slice(qb * QB, (qb + 1) * QB)
            depth, base = (qb + 1) * QB, strip_offset(qb)
            d_scores = p_s[h, base:base + depth, :]
            add_k = dot(qT[rows, cols], d_scores, 1, 1)
            if qb == NQ - 1:
                dacc_k[:, 0:depth] = add_k
            else:
                dacc_k[:, 0:depth] += add_k
            yield
            d_query = dot(kT[rows, 0:depth], d_scores, 1, 0) * HD ** -0.5
            side, lane = divmod(qb * QB, half)
            parts[0][pl.ds(pl.multiple_of(side * Dh + h * HD, HD), HD), lane:lane + QB] = unrotated(
                d_query.astype(bf16).astype(f32), cos_s[:, cols], sin_s[:, cols]
            ).astype(bf16)
            yield

        for _ in score_back(NQ - 1):
            pass
        for qb in reversed(range(NQ)):
            interleave(score_back(qb - 1) if qb else iter(()), qb + 1 if qb else 0, spread_back(qb), 2)
        for side in range(2):
            cols = slice(side * half, (side + 1) * half)
            place_rows = pl.ds(pl.multiple_of(side * Dh + h * HD, HD), HD)
            parts[1][place_rows, 0:half] = unrotated(
                dacc_k[:, cols].astype(bf16).astype(f32), cos_s[:, cols], sin_s[:, cols]
            ).astype(bf16)
            parts[2][place_rows, 0:half] = dacc_v[:, cols].astype(bf16)
        @pl.when(h == 0)
        def _():
            advance(a4)

        @pl.when(h == 1)
        def _():
            advance(a1, a2)
            lin_grads(0)
            b1.begin()

        @pl.when(h == 2)
        def _():
            advance(a4, a3, a1, a2)

    advance(a1, b1)

    def back_norm(side, start):
        side_rows = pl.ds(pl.multiple_of(side * Dh, Dh), Dh)
        total = None
        for i in range(3):
            term = dot(parts[i][side_rows, pl.ds(start, MB)], wqkvT[i * Dh:(i + 1) * Dh, :], 0, 0)
            total = term if total is None else total + term
        return total

    @pl.loop(0, half // MB)
    def _(i):
        start = pl.multiple_of(i * MB, MB)
        nm[pl.ds(start, MB), :] = back_norm(1 - c, start).astype(bf16)

    dn_in = cots
    dn_copy = remote(nm, dn_in, dn_send.at[0], dn_recv.at[0], sib, z)
    dn_copy.start()
    advance(a2, a4, a3)
    lin_grads(1)
    advance(a1)
    back_wait(xs, (1 - c) * half, out, out_send, out_recv, loc_sem.at[pl.ds(2, per)])
    dn_copy.wait()

    g_ga[...] = jnp.zeros((8, D), f32)

    @pl.loop(0, NB)
    def _(i):
        start = pl.multiple_of(i * MB, MB)
        rows = pl.ds(start, MB)
        own = pl.ds(pl.multiple_of(c * half + start, MB), MB)
        d_normed = back_norm(c, start) + dn_in[rows, :].astype(f32)
        plain, inverse = rms(xs[own, :].astype(f32))
        scaled = d_normed * gain_a[...]
        g_ga[...] += fold_rows(d_normed * plain)
        d_start = inverse * (scaled - plain * jnp.mean(scaled * plain, axis=-1, keepdims=True))
        nm[rows, :] = (da[rows, :].astype(f32) + d_start).astype(bf16)

        @pl.when(i == 1)
        def _():
            advance(b1, a4)

        @pl.when(i == 2)
        def _():
            advance(a2, a3)

    advance(a1)
    for k in range(D // quarter):
        features = slice(k * quarter, (k + 1) * quarter)
        gB[3 * D + 8 * k:3 * D + 8 * (k + 1), side_cols[1]] = g_ga[:, features].astype(bf16)
    b2.begin()
    for step in SCHEDULE:
        if step < 6:
            sums[step].advance()
        else:
            i = jnp.int32(step - 6)
            back_start(i, nm, i * MB, gin, gin_send, gin_recv, loc_sem.at[pl.ds(2 + per, per)])
    back_wait(nm, 0, gin, gin_send, gin_recv, loc_sem.at[pl.ds(2 + per, per)])


def on_device(
    G, S, NP,
    inputs, segment_ids, cotangent, norm_attn, norm_mlp, w_query, w_key, w_value, w_out, w_gate, w_up, w_down,
):
    _, T, D = inputs.shape
    FF = w_gate.shape[1]
    L = T * S
    half, Dh = L // 2, D // 2
    NH = Dh // HD
    anywhere = pl.BlockSpec(memory_space=pl.ANY)
    vmem = pl.BlockSpec(memory_space=pltpu.VMEM)
    dma = pltpu.SemaphoreType.DMA

    def buf(*shape, dtype=bf16):
        return pltpu.VMEM(shape, dtype)

    strips = strip_offset(L // QB)
    shards = NP * S
    RA, RB = padded(3 * FF + D + 16, shards), padded(3 * D + 32, shards)

    sizes = axis_sizes(NP, S)
    scattered = [(count, sizes[k % 2], True, Dh) for k, (_, count) in enumerate(split_rows(RA, FF, 2 * FF, shards))]
    scattered += [(RB, sizes[2], False, Dh // 2)] * 2
    sum_scratch = []
    for count, over, core, width in scattered:
        sum_scratch += [buf(*shape) for shape in lands(count, over, core, width)]
        sum_scratch += [dma((copies_of(over),)), dma((copies_of(over),))]
    NB, per = half // MB, T // MB
    out, gin, out_a, out_b = pl.pallas_call(
        functools.partial(block_kernel, G, S, NP, T, L, D, FF),
        out_shape=[
            jax.ShapeDtypeStruct((G, T, D), bf16),
            jax.ShapeDtypeStruct((G, T, D), bf16),
            jax.ShapeDtypeStruct((RA, D), bf16),
            jax.ShapeDtypeStruct((RB, D), bf16),
        ],
        in_specs=[anywhere, vmem, anywhere, vmem, vmem] + [anywhere] * 7,
        out_specs=[anywhere] * 4,
        scratch_shapes=[
            buf(L, D), buf(half, D), buf(G, L, dtype=jnp.int32), buf(8, L, dtype=f32),
            buf(HD // 2, L, dtype=f32), buf(HD // 2, L, dtype=f32),
            buf(L, D), buf(3 * Dh, D), buf(RA, D), buf(RB, D),
            buf(Dh, L), buf(Dh, L), buf(Dh, L),
            buf(NH, strips, QB), buf(2, L, QB, dtype=f32), buf(NH, 8, L, dtype=f32), buf(Dh, L), buf(D, half),
            buf(half, D), buf(half, FF), buf(half, FF), buf(half, FF),
            buf(half, D), buf(D, half),
            buf(Dh, L), buf(HD, L, dtype=f32), buf(HD, L, dtype=f32),
            buf(8, D, dtype=f32), buf(8, D, dtype=f32),
            dma((7,)), dma((2 + 2 * per,)), dma((2,)), dma((G,)), dma((S,)), dma((S,)), dma((G,)), dma((G,)),
            dma((NH,)), dma((NH,)), dma((NB,)), dma((G * per,)), dma((1,)), dma((1,)), dma((1,)), dma((1,)),
            dma((NB,)), dma((G * per,)), dma((6,)),
            *sum_scratch,
        ],
        compiler_params=pltpu.CompilerParams(
            collective_id=0, has_side_effects=True, vmem_limit_bytes=63 * 2**20
        ),
    )(
        inputs, segment_ids, cotangent, norm_attn.reshape(1, D), norm_mlp.reshape(1, D),
        w_query, w_key, w_value, w_out, w_gate.T, w_up.T, w_down,
    )

    moves = []
    for k in range(3):
        moves += [(1, k * FF + first, FF // 2, k, first) for first in (0, FF // 2)]
    moves.append((1, 3 * FF, D, 3, 0))
    moves += [(2, k * D, D, 4 + k, 0) for k in range(3)]
    moves += [(3, l * T, T, 7, l * T) for l in range(G)]

    def convert_kernel(out_ref, a_ref, b_ref, gin_ref, *rest):
        targets = rest[:8]
        final_out, gain_a_out, gain_m_out = rest[8:11]
        scratch = rest[11:]
        lows, wides = scratch[:len(moves)], scratch[len(moves):2 * len(moves)]
        tail_a, tail_b, out_low, read, write = scratch[2 * len(moves):]
        sources = (out_ref, a_ref, b_ref, gin_ref)
        last = len(moves)
        extra = [
            pltpu.make_async_copy(a_ref.at[pl.ds(3 * FF + D, 16)], tail_a, read.at[last]),
            pltpu.make_async_copy(b_ref.at[pl.ds(3 * D, 32)], tail_b, read.at[last + 1]),
            pltpu.make_async_copy(out_ref, out_low, read.at[last + 2]),
        ]
        reads, writes = [], []
        for k, (source, row, rows, target, to) in enumerate(moves):
            reads.append(pltpu.make_async_copy(sources[source].at[pl.ds(row, rows)], lows[k], read.at[k]))
            writes.append(pltpu.make_async_copy(wides[k], targets[target].at[pl.ds(to, rows)], write.at[k]))
        for copy in reads + extra:
            copy.start()
        for k in range(len(moves)):
            reads[k].wait()
            wides[k][...] = lows[k][...].astype(f32)
            writes[k].start()
        for copy in extra:
            copy.wait()
        final = pltpu.make_async_copy(out_low, final_out, write.at[last])
        final.start()
        gain_m_out[...] = jnp.sum(tail_a[0:8, :].astype(f32), axis=0)
        tail = tail_b[:, Dh // 2:Dh].astype(f32) + tail_b[:, Dh + Dh // 2:].astype(f32)
        gains = [jnp.sum(tail[8 * k:8 * (k + 1)], axis=0, keepdims=True) for k in range(4)]
        gain_a_out[...] = jnp.concatenate(gains, axis=1).reshape(D)
        for copy in writes + [final]:
            copy.wait()

    full = [(FF, D)] * 3 + [(D, D)] * 4 + [(G * T, D)]
    results = pl.pallas_call(
        convert_kernel,
        out_shape=[jax.ShapeDtypeStruct(shape, f32) for shape in full]
        + [jax.ShapeDtypeStruct((G * T, D), bf16), jax.ShapeDtypeStruct((D,), f32), jax.ShapeDtypeStruct((D,), f32)],
        in_specs=[anywhere] * 4,
        out_specs=[anywhere] * 9 + [vmem, vmem],
        scratch_shapes=[buf(move[2], D) for move in moves] + [buf(move[2], D, dtype=f32) for move in moves]
        + [buf(16, D), buf(32, D), buf(G * T, D), dma((len(moves) + 3,)), dma((len(moves) + 1,))],
        compiler_params=pltpu.CompilerParams(vmem_limit_bytes=62 * 2**20),
    )(out.reshape(G * T, D), out_a, out_b, gin.reshape(G * T, D))
    g_gate, g_up, g_down, g_out, g_query, g_key, g_value, grad_input, output, gain_attn, gain_mlp = results
    return (
        output.reshape(G, T, D), grad_input.reshape(G, T, D), gain_attn, gain_mlp,
        g_query, g_key, g_value, g_out, g_gate.T, g_up.T, g_down,
    )


def solution(mesh):
    S = mesh.shape["seq"]
    NP = mesh.shape["dp"] // 2
    rows = P("dp", "seq", None)
    return jax.shard_map(
        functools.partial(on_device, S // 2, S, NP),
        mesh=mesh,
        in_specs=(rows, P("dp", None), rows) + (P(),) * 9,
        out_specs=(rows, rows) + (P(),) * 9,
        check_vma=False,
    )
```

```python
import functools

import jax
import jax.numpy as jnp
from jax import lax
from jax.experimental import pallas as pl
from jax.experimental.pallas import tpu as pltpu
from jax.sharding import PartitionSpec as P

HD = 64
DOCS = 7
epsilon = 1e-05
theta_base = 10000.0
masked_value = -1e30
MESH = pl.DeviceIdType.MESH
f32 = jnp.float32
bf16 = jnp.bfloat16
QB = 256
MB = 256
AXES = ("xynf", "yxnf", "xynf", "yxnf", "pz", "pz")
CUT = 1
SCHEDULE = {
    "down": (0,),
    "grads": (1, 2),
    "head 0": (3,),
    "head 1": (0, 1),
    "head 2": (3, 2, 0, 1),
    "head 3": (0, 4),
    "parts": (1, 3, 2),
    "projections": (0,),
    "gin 1": (4, 3),
    "gin 2": (1, 2),
    "gin 3": (0,),
    "end": (4, 3, 1, 0, 2, 5, 3, 1, 2, 4, 3, 5, 4, 2, 0, 1, 6, 3, 2, 7, 5, 0, 8, 0, 1, 1, 9, 2, 3, 2, 3, 5, 5),
}
EDGE = 128


def dot(left, right, left_dim, right_dim):
    return lax.dot_general(
        left, right, (((left_dim,), (right_dim,)), ((), ())), preferred_element_type=f32
    )


def strip_offset(block):
    return QB * block * (block + 1) // 2


def padded(rows, shards):
    unit = 16 * shards
    return (rows + unit - 1) // unit * unit


class Axis:
    def __init__(self, size, index, device):
        self.size, self.index, self.device = size, index, device

    def others(self):
        return [lax.rem(self.index + k, self.size) for k in range(1, self.size)]


def lands(rows, sizes, core, width):
    shapes = [(rows, width)] if core else []
    for size in sizes:
        rows //= size
        shapes.append((size - 1, rows, width))
    return shapes


def copies_of(sizes):
    return 2 + 2 * sum(size - 1 for size in sizes)


class Total:
    def __init__(self, remote, core, axes, own, other, buf, result, local, base, count, land, send, recv):
        self.remote, self.core, self.axes, self.own, self.other = remote, core, axes, own, other
        self.buf, self.result, self.local = buf, result, local
        self.base, self.count = base, count
        self.send, self.recv = send, recv
        sizes = [axis.size for axis in axes]
        self.with_core = len(land) > len(sizes)
        self.land = list(land)
        self.starts, self.counts, self.first_sem = [base], [count], [2]
        for axis in axes:
            self.counts.append(self.counts[-1] // axis.size)
            self.starts.append(self.starts[-1] + axis.index * self.counts[-1])
            self.first_sem.append(self.first_sem[-1] + 2 * (axis.size - 1))
        self.stages = [("core", 0)] if self.with_core else []
        self.stages += [("scatter", k) for k in range(len(axes))]
        self.stages += [("gather", k) for k in reversed(range(len(axes)))]
        self.stages.append(("back", 0))
        self.at = 0

    def rows(self, start, count):
        return pl.ds(pl.multiple_of(start, 16), count)

    def copies(self, stage):
        kind, k = stage
        if kind == "core":
            src = self.buf.at[pl.ds(self.base, self.count), self.other]
            return [self.remote(src, self.land[0], self.send.at[0], self.recv.at[0], *self.core)]
        if kind == "back":
            half = self.result.at[pl.ds(self.base, self.count), self.own]
            return [self.remote(half, half, self.send.at[1], self.recv.at[1], *self.core)]
        axis, count = self.axes[k], self.counts[k + 1]
        land = self.land[k + self.with_core]
        made = []
        for slot, to in enumerate(axis.others()):
            if kind == "scatter":
                src = self.buf.at[self.rows(self.starts[k] + to * count, count), self.own]
                dst, sem = land.at[slot], self.first_sem[k] + slot
            else:
                rows = self.rows(self.starts[k + 1], count)
                source = self.buf if k == len(self.axes) - 1 else self.result
                src, dst = source.at[rows, self.own], self.result.at[rows, self.own]
                sem = self.first_sem[k] + axis.size - 1 + slot
            made.append(self.remote(src, dst, self.send.at[sem], self.recv.at[sem], *axis.device(to)))
        if kind == "gather" and k == len(self.axes) - 1:
            rows = self.rows(self.starts[k + 1], count)
            made.append(pltpu.make_async_copy(self.buf.at[rows, self.own], self.result.at[rows, self.own], self.local))
        return made

    def add(self, start, count, land):
        chunk = self.counts[-1]

        @pl.loop(0, count // chunk)
        def _(i):
            rows = self.rows(start + i * chunk, chunk)
            total = self.buf[rows, self.own].astype(f32)
            for piece in land:
                total = total + piece[self.rows(i * chunk, chunk), :].astype(f32)
            self.buf[rows, self.own] = total.astype(bf16)

    def begin(self):
        for copy in self.copies(self.stages[self.at]):
            copy.start()

    def advance(self):
        kind, k = stage = self.stages[self.at]
        for copy in self.copies(stage):
            copy.wait()
        if kind == "core":
            self.add(self.base, self.count, [self.land[0]])
        elif kind == "scatter":
            land = self.land[k + self.with_core]
            self.add(self.starts[k + 1], self.counts[k + 1], [land.at[slot] for slot in range(self.axes[k].size - 1)])
        self.at += 1
        if self.at < len(self.stages):
            self.begin()


def fold_rows(values):
    rows, width = values.shape
    return jnp.sum(values.reshape(rows // 8, 8, width), axis=0)


def sum_rows(RA, RB, D, FF, shards):
    unit = 16 * shards
    edges = [0, FF // unit * unit, 2 * FF // unit * unit]
    edges += [min((edges[2] + RA + CUT * unit) // 2 // unit, 3 * FF // unit) * unit, RA]
    return [(start, end - start) for start, end in zip(edges, edges[1:])] + [(0, padded(3 * D, shards)), (0, RB)]


def axis_sizes(NP, S):
    fast = 2 if NP % 2 == 0 else 1
    return {"x": fast, "y": NP // fast, "n": 2, "f": S // 2, "p": NP, "z": S}


def interleave(main, count_main, side, count_side):
    steps = max(count_main, count_side)
    done_main = done_side = 0
    for step in range(1, steps + 1):
        while done_main < step * count_main / steps:
            next(main, None)
            done_main += 1
        while done_side < step * count_side / steps:
            next(side, None)
            done_side += 1
    for _ in main:
        pass
    for _ in side:
        pass


def block_kernel(
    G, S, NP, T, L, D, FF,
    x, seg, cot, gain_a, gain_m, wq, wk, wv, wo, wgT, wuT, wd,
    out, gin, out_a, out_b,
    xs, cots, seg_other, first_s, cos_s, sin_s, n_s, wqkvT, gA, gB,
    qT, kT, vT, p_s, s_buf, inv_tot, mixT, mfull, nm, hid, dga, dup, da, dmT,
    dOT, dacc_k, dacc_v, g_ga, g_gm,
    w_sem, loc_sem, seg_sem, x_send, x_recv, fwd_send, cot_send, cot_recv, mix_send, mix_recv,
    out_send, out_recv, dm_send, dm_recv, dn_send, dn_recv, gin_send, gin_recv, g_sem,
    *rest,
):
    d = lax.axis_index("dp")
    z = lax.axis_index("seq")
    c = lax.rem(d, 2)
    pair = d - c
    sib = pair + 1 - c
    gz = z // G
    lz = lax.rem(z, G)
    half = L // 2
    Dh = D // 2
    NH = Dh // HD

    def remote(src, dst, send, recv, dp, seq):
        return pltpu.make_async_remote_copy(
            src_ref=src, dst_ref=dst, send_sem=send, recv_sem=recv,
            device_id=(dp, seq), device_id_type=MESH,
        )

    own_cols = pl.ds(pl.multiple_of(c * Dh, Dh), Dh)
    other_cols = pl.ds(pl.multiple_of((1 - c) * Dh, Dh), Dh)
    pr = d // 2
    fast = 2 if NP % 2 == 0 else 1
    row_at, col_at = pr // fast, lax.rem(pr, fast)
    low, high = lax.rem(z, 2), z // 2
    axes = {
        "x": Axis(fast, col_at, lambda j: (2 * (row_at * fast + j) + c, z)),
        "y": Axis(NP // fast, row_at, lambda j: (2 * (j * fast + col_at) + c, z)),
        "n": Axis(2, low, lambda j: (d, high * 2 + j)),
        "f": Axis(S // 2, high, lambda j: (d, j * 2 + low)),
        "p": Axis(NP, pr, lambda j: (2 * j + c, z)),
        "z": Axis(S, z, lambda j: (d, j)),
    }
    rest = list(rest)

    def take(count):
        taken = rest[:count]
        del rest[:count]
        return taken

    quarter = Dh // 2
    side_cols = [pl.ds(pl.multiple_of(c * Dh + k * quarter, quarter), quarter) for k in range(2)]
    sums = []
    for k, (base, count) in enumerate(sum_rows(gA.shape[0], gB.shape[0], D, FF, NP * S)):
        core = k < 4
        over = [axes[letter] for letter in AXES[k]]
        land = take(len(over) + core)
        send, recv = take(2)
        sums.append(Total(
            remote, (sib, z), over, own_cols if core else side_cols[k - 4], other_cols, gA if core else gB,
            out_a if core else out_b, g_sem.at[k], base, count, land, send, recv,
        ))
    a1, a2, a3, a4, b1, b2 = sums

    def step_at(place):
        for each in SCHEDULE[place]:
            sums[each].advance()

    up_row, down_row, out_row, gain_row = FF, 2 * FF, 3 * FF, 3 * FF + D

    loads = [
        pltpu.make_async_copy(w.at[:, own_cols], gB.at[pl.ds(i * D, D), own_cols], w_sem.at[i])
        for i, w in enumerate((wq, wk, wv))
    ] + [
        pltpu.make_async_copy(wgT, gA.at[pl.ds(0, FF)], w_sem.at[3]),
        pltpu.make_async_copy(wuT, gA.at[pl.ds(up_row, FF)], w_sem.at[4]),
        pltpu.make_async_copy(wd, gA.at[pl.ds(down_row, FF)], w_sem.at[5]),
        pltpu.make_async_copy(wo, gA.at[pl.ds(out_row, D)], w_sem.at[6]),
    ]
    for load in loads:
        load.start()
    for buffer, used in ((gA, gain_row), (gB, 3 * D)):
        buffer[used:buffer.shape[0], :] = jnp.zeros((buffer.shape[0] - used, D), bf16)
    wo_s = gA.at[pl.ds(out_row, D)]

    barrier = pltpu.get_barrier_semaphore()
    for step in range(1, 2 * S):
        other = lax.rem(c * S + z + step, 2 * S)
        pl.semaphore_signal(
            barrier, inc=1, device_id=(pair + other // S, lax.rem(other, S)), device_id_type=MESH
        )
    for step in range(1, NP):
        pl.semaphore_signal(
            barrier, inc=1, device_id=(2 * lax.rem(pr + step, NP) + c, z), device_id_type=MESH
        )
    pl.semaphore_wait(barrier, 2 * S - 1 + NP - 1)

    seg_copy = remote(seg, seg_other, seg_sem.at[0], seg_sem.at[1], sib, z)
    seg_copy.start()

    def x_rows(index):
        return xs.at[pl.ds(pl.multiple_of(index * T, T), T)]

    def x_copy(l):
        return remote(x.at[l], x_rows(z), x_send.at[l], x_recv.at[z], d, c * G + l)

    own_x = pltpu.make_async_copy(x.at[lz], x_rows(z), loc_sem.at[0])
    own_fwd = remote(x.at[lz], x_rows(z), fwd_send.at[0], x_recv.at[z], sib, z)

    @pl.when(gz == c)
    def _():
        own_x.start()
        own_fwd.start()

    for l in range(G):
        @pl.when(c * G + l != z)
        def _():
            x_copy(l).start()

    for load in loads:
        load.wait()
    for i in range(3):
        wqkvT[i * Dh:(i + 1) * Dh, :] = gB[i * D:(i + 1) * D, own_cols].T
    seg_copy.wait()
    seg_mine = jnp.where(gz == c, seg[...], seg_other[...])
    row = jnp.zeros((1, L), jnp.int32)
    for l in range(G):
        row = jnp.where(lz == l, seg_mine[l:l + 1, :], row)
    ids = row.astype(f32)
    first = jnp.zeros((1, L), f32)
    for doc in range(1, DOCS):
        before = jnp.sum(jnp.where(ids < doc, 1.0, 0.0), axis=1, keepdims=True)
        first = jnp.where(ids >= doc, before, first)
    first_s[...] = jnp.broadcast_to(first, (8, L))
    token = lax.broadcasted_iota(jnp.int32, (1, L), 1).astype(f32)
    place = token - first
    order = lax.broadcasted_iota(jnp.int32, (HD // 2, 1), 0).astype(f32)
    frequency = jnp.exp(order * f32(-2.0 * 9.210340371976184 / HD))
    angle = place * frequency
    cos_s[...] = jnp.cos(angle)
    sin_s[...] = jnp.sin(angle)

    def rms(values):
        inverse = lax.rsqrt(jnp.mean(values * values, axis=-1, keepdims=True) + epsilon)
        return values * inverse, inverse

    def project(start, size):
        rows = pl.ds(start, size)
        plain, _ = rms(xs[rows, :].astype(f32))
        normed = (plain * gain_a[...]).astype(bf16)
        n_s[rows, :] = normed
        lin = dot(wqkvT[...], normed, 1, 1)
        cosine, sine = cos_s[:, rows], sin_s[:, rows]

        def rotated(base):
            parts = []
            for h in range(NH):
                a = lin[base + h * HD:base + h * HD + HD // 2]
                b = lin[base + h * HD + HD // 2:base + (h + 1) * HD]
                parts.append(jnp.concatenate([a * cosine - b * sine, b * cosine + a * sine], axis=0))
            return parts

        query = jnp.concatenate(rotated(0), axis=0).astype(bf16)
        qT[:, rows] = (query.astype(f32) * HD ** -0.5).astype(bf16)
        kT[:, rows] = jnp.concatenate(rotated(Dh), axis=0).astype(bf16)
        vT[:, rows] = lin[2 * Dh:].astype(bf16)

    def with_flipped(value, step):
        bits = [lax.rem(value // 2 ** k, 2) for k in range(S.bit_length() - 1)]
        return sum(2 ** k * (1 - bit if step // 2 ** k % 2 else bit) for k, bit in enumerate(bits))

    for step in range(S):
        source = with_flipped(z, step)
        arrived = remote(x.at[0], x_rows(source), x_send.at[0], x_recv.at[source], sib, z)
        if step == 0:
            @pl.when(gz == c)
            def _():
                own_x.wait()

            @pl.when(gz != c)
            def _():
                arrived.wait_recv()
        else:
            arrived.wait_recv()

            @pl.when(gz == c)
            def _():
                remote(x_rows(source), x_rows(source), fwd_send.at[step], x_recv.at[source], sib, z).start()

        @pl.loop(0, T // QB)
        def _(i):
            project(pl.multiple_of(source * T + i * QB, QB), QB)

    for l in range(G):
        @pl.when(c * G + l != z)
        def _():
            x_copy(l).wait_send()

    @pl.when(gz == c)
    def _():
        own_fwd.wait_send()
        for step in range(1, S):
            remote(x.at[0], x_rows(z), fwd_send.at[step], x_recv.at[z], sib, z).wait_send()

    to_core = z // G
    slot = lax.rem(z, G)

    def cot_rows(index):
        return cots.at[pl.ds(pl.multiple_of(index * T, T), T)]

    def cot_copy(l):
        return remote(cot.at[l], cot_rows(slot), cot_send.at[l], cot_recv.at[slot], pair + to_core, c * G + l)

    own_cot = pltpu.make_async_copy(cot.at[lz], cot_rows(slot), loc_sem.at[1])
    keeps_own = (gz == c) & (to_core == c)
    for l in range(G):
        here = (c * G + l == z) & (to_core == c)

        @pl.when(jnp.logical_not(here))
        def _():
            cot_copy(l).start()

    @pl.when(keeps_own)
    def _():
        own_cot.start()

    NQ = L // QB

    def place_of(rows, first_row):
        return (lax.broadcasted_iota(jnp.int32, (rows, QB), 0) + first_row).astype(f32)

    def mask_of(tile, qb, kb):
        begin = first_s[0:1, qb * QB:(qb + 1) * QB]
        query_place = (lax.broadcasted_iota(jnp.int32, (1, QB), 1) + qb * QB).astype(f32)
        edge = qb in (0, NQ - 1)
        if edge:
            tile = jnp.where(place_of(QB, kb * QB) >= begin, tile, masked_value)
        elif kb == 0:
            head = jnp.where(place_of(EDGE, 0) >= begin, tile[:EDGE], masked_value)
            tile = jnp.concatenate([head, tile[EDGE:]], axis=0)
        if kb == qb:
            tile = jnp.where(place_of(QB, kb * QB) <= query_place, tile, masked_value)
        return tile

    def mix_copy(h):
        return remote(
            mixT.at[pl.ds(pl.multiple_of(h * HD, HD), HD), pl.ds(pl.multiple_of((1 - c) * half, half), half)],
            mfull.at[pl.ds(pl.multiple_of(c * Dh + h * HD, HD), HD), :],
            mix_send.at[h], mix_recv.at[h], sib, z,
        )

    order = [1] + list(range(NQ - 1, 1, -1)) + [0]

    @pl.loop(0, NH)
    def _(h):
        rows = pl.ds(pl.multiple_of(h * HD, HD), HD)
        tops = {}

        def score(turn):
            qb = order[turn]
            query = qT[rows, qb * QB:(qb + 1) * QB]
            top = None
            for kb in range(qb + 1):
                tile = mask_of(dot(kT[rows, kb * QB:(kb + 1) * QB], query, 0, 0), qb, kb)
                part = jnp.max(tile.reshape(QB // 8, 8, QB), axis=0)
                top = part if top is None else jnp.maximum(top, part)
                s_buf[turn % 2, kb * QB:(kb + 1) * QB, :] = tile
                yield
            tops[turn] = jnp.max(top, axis=0, keepdims=True)

        def weigh(turn):
            qb = order[turn]
            cols = slice(qb * QB, (qb + 1) * QB)
            depth, base = (qb + 1) * QB, strip_offset(qb)
            total = None
            for kb in range(qb + 1):
                expanded = jnp.exp(s_buf[turn % 2, kb * QB:(kb + 1) * QB, :] - tops[turn])
                part = jnp.sum(expanded.reshape(QB // 8, 8, QB), axis=0)
                total = part if total is None else total + part
                p_s[h, base + kb * QB:base + (kb + 1) * QB, :] = expanded.astype(bf16)
                yield
            inverse = 1.0 / jnp.sum(total, axis=0, keepdims=True)
            inv_tot[h, :, cols] = jnp.broadcast_to(inverse, (8, QB))
            low = p_s[h, base:base + depth, :]
            mixT[rows, cols] = (dot(vT[rows, 0:depth], low, 1, 0) * inverse).astype(bf16)

        for _ in score(0):
            pass
        for turn, qb in enumerate(order):
            more = turn + 1 < len(order)
            interleave(
                score(turn + 1) if more else iter(()), order[turn + 1] + 1 if more else 0, weigh(turn), qb + 1
            )
        mix_copy(h).start()
        mfull[pl.ds(pl.multiple_of(c * Dh + h * HD, HD), HD), :] = mixT[
            rows, pl.ds(pl.multiple_of(c * half, half), half)
        ]

    @pl.loop(0, NH)
    def _(h):
        mix_copy(h).wait_send()
        remote(
            mixT.at[0:HD, 0:half], mfull.at[pl.ds(pl.multiple_of((1 - c) * Dh + h * HD, HD), HD), :],
            mix_send.at[h], mix_recv.at[h], sib, z,
        ).wait_recv()

    own_rows = pl.ds(pl.multiple_of(c * Dh, Dh), Dh)

    ff_cuts = [(first_col, min(first_col + 512, FF)) for first_col in range(0, FF, 512)]
    g_gm[...] = jnp.zeros((8, D), f32)
    NB = half // MB
    per = T // MB

    def back_copy(i, src, row, dst, send, recv):
        inside = pl.ds(pl.multiple_of(lax.rem(i, per) * MB, MB), MB)
        return remote(
            src.at[pl.ds(pl.multiple_of(row, MB), MB)], dst.at[lz, inside],
            send.at[i], recv.at[lz * per + lax.rem(i, per)], pair + gz, c * G + i // per,
        )

    def back_local(i, src, row, dst, local):
        inside = pl.ds(pl.multiple_of(lax.rem(i, per) * MB, MB), MB)
        return pltpu.make_async_copy(src.at[pl.ds(pl.multiple_of(row, MB), MB)], dst.at[lz, inside], local.at[lax.rem(i, per)])

    def stays(i):
        return (gz == c) & (c * G + i // per == z)

    def back_start(i, src, row, dst, send, recv, local):
        @pl.when(jnp.logical_not(stays(i)))
        def _():
            back_copy(i, src, row, dst, send, recv).start()

        @pl.when(stays(i))
        def _():
            back_local(i, src, row, dst, local).start()

    def back_wait(src, row, dst, send, recv, local):
        @pl.loop(0, NB)
        def _(i):
            @pl.when(jnp.logical_not(stays(i)))
            def _():
                back_copy(i, src, row + i * MB, dst, send, recv).wait_send()

            @pl.when(stays(i))
            def _():
                back_local(i, src, row + i * MB, dst, local).wait()
        for l in range(G):
            mine = (c * G + l == z) & (gz == c)
            for part in range(per):
                @pl.when(jnp.logical_not(mine))
                def _():
                    remote(
                        src.at[pl.ds(0, MB)], dst.at[l, pl.ds(part * MB, MB)],
                        send.at[0], recv.at[l * per + part], sib, z,
                    ).wait_recv()

    @pl.loop(0, NB)
    def _(i):
        start = pl.multiple_of(i * MB, MB)
        rows = pl.ds(start, MB)
        base = xs[pl.ds(pl.multiple_of(c * half + start, MB), MB), :].astype(f32)
        middle = base + dot(mfull[:, rows], wo_s[...], 0, 0)
        da[rows, :] = middle.astype(bf16)
        plain, _ = rms(middle)
        normed = (plain * gain_m[...]).astype(bf16)
        nm[rows, :] = normed
        result = middle
        for first_col, last_col in ff_cuts:
            cut = slice(first_col, last_col)
            cut_up = slice(up_row + first_col, up_row + last_col)
            cut_down = slice(down_row + first_col, down_row + last_col)
            gate = dot(normed, gA[cut, :], 1, 1)
            up = dot(normed, gA[cut_up, :], 1, 1)
            dga[rows, cut] = gate.astype(bf16)
            dup[rows, cut] = up.astype(bf16)
            hidden = (gate / (1.0 + jnp.exp(-gate)) * up).astype(bf16)
            hid[rows, cut] = hidden
            result = result + dot(hidden, gA[cut_down, :], 1, 0)
        spare = pl.multiple_of((1 - c) * half + start, MB)
        xs[pl.ds(spare, MB), :] = result.astype(bf16)
        back_start(i, xs, spare, out, out_send, out_recv, loc_sem.at[pl.ds(2, per)])

    @pl.loop(0, NB)
    def _(i):
        start = pl.multiple_of(i * MB, MB)
        rows = pl.ds(start, MB)
        mine = stays(i)

        @pl.when((lax.rem(i, per) == 0) & jnp.logical_not(mine))
        def _():
            remote(cot.at[0], cot_rows(i // per), cot_send.at[0], cot_recv.at[i // per], sib, z).wait_recv()

        @pl.when((lax.rem(i, per) == 0) & mine)
        def _():
            own_cot.wait()

        plain, inverse = rms(da[rows, :].astype(f32))
        grad = cots[rows, :]
        d_normed = None
        for first_col, last_col in ff_cuts:
            cut = slice(first_col, last_col)
            cut_up = slice(up_row + first_col, up_row + last_col)
            cut_down = slice(down_row + first_col, down_row + last_col)
            gate, up = dga[rows, cut].astype(f32), dup[rows, cut].astype(f32)
            sig = 1.0 / (1.0 + jnp.exp(-gate))
            d_hidden = dot(grad, gA[cut_down, :], 1, 1)
            d_gate = (d_hidden * up * sig * (1.0 + gate * (1.0 - sig))).astype(bf16)
            d_up = (d_hidden * (gate * sig)).astype(bf16)
            dga[rows, cut] = d_gate
            dup[rows, cut] = d_up
            term = dot(d_gate, gA[cut, :], 1, 0) + dot(d_up, gA[cut_up, :], 1, 0)
            d_normed = term if d_normed is None else d_normed + term
        scaled = d_normed * gain_m[...]
        g_gm[...] += fold_rows(d_normed * plain)
        d_middle = grad.astype(f32) + inverse * (scaled - plain * jnp.mean(scaled * plain, axis=-1, keepdims=True))
        d_attn = d_middle.astype(bf16)
        da[rows, :] = d_attn
        dmT[:, rows] = dot(wo_s[...], d_attn, 1, 1).astype(bf16)

    dm_copy = remote(
        dmT.at[pl.ds(pl.multiple_of((1 - c) * Dh, Dh), Dh), :],
        dOT.at[:, pl.ds(pl.multiple_of(c * half, half), half)], dm_send.at[0], dm_recv.at[0], sib, z
    )
    dm_copy.start()

    for l in range(G):
        here = (c * G + l == z) & (to_core == c)

        @pl.when(jnp.logical_not(here))
        def _():
            cot_copy(l).wait_send()

    def ff_grad(target, base, left, right):
        for first_row in range(0, FF, 512):
            last_row = min(first_row + 512, FF)
            grad = dot(left[:, first_row:last_row], right[...], 0, 0)
            target[base + first_row:base + last_row, :] = grad.astype(bf16)

    ff_grad(gA, 0, dga, nm)
    a1.begin()
    ff_grad(gA, up_row, dup, nm)
    a2.begin()
    ff_grad(gA, down_row, hid, cots)
    a3.begin()
    step_at("down")
    gA[out_row:out_row + D, :] = dot(mfull[...], da[...], 1, 0).astype(bf16)
    gA[gain_row:gain_row + 16, :] = jnp.concatenate([g_gm[...], jnp.zeros((8, D), f32)], axis=0).astype(bf16)
    a4.begin()
    step_at("grads")

    dm_copy.wait()
    dOT[:, pl.ds(pl.multiple_of(c * half, half), half)] = dmT[own_rows, :]
    parts = (dga, dup, hid)

    def lin_grads(side):
        rows = slice(side * quarter, (side + 1) * quarter)
        late = slice(Dh + side * quarter, Dh + (side + 1) * quarter)
        for i in range(3):
            grad = dot(parts[i][rows, 0:half], n_s[0:half, :], 1, 0)
            grad = grad + dot(parts[i][late, 0:half], n_s[half:L, :], 1, 0)
            gB[i * D:(i + 1) * D, side_cols[side]] = grad.T.astype(bf16)

    def unrotated(values, cosine, sine):
        a, b = values[:HD // 2], values[HD // 2:]
        return jnp.concatenate([a * cosine + b * sine, b * cosine - a * sine], axis=0)

    @pl.loop(0, NH)
    def _(h):
        rows = pl.ds(pl.multiple_of(h * HD, HD), HD)

        def score_back(qb):
            cols = slice(qb * QB, (qb + 1) * QB)
            depth, base = (qb + 1) * QB, strip_offset(qb)
            grad_wide = dOT[rows, cols].astype(f32) * inv_tot[h, 0:1, cols]
            delta = jnp.sum(grad_wide * mixT[rows, cols].astype(f32), axis=0, keepdims=True)
            grad = grad_wide.astype(bf16)
            add_v = dot(grad, p_s[h, base:base + depth, :], 1, 1)
            if qb == NQ - 1:
                dacc_v[:, 0:depth] = add_v
            else:
                dacc_v[:, 0:depth] += add_v
            yield
            for kb in range(qb + 1):
                tile = slice(base + kb * QB, base + (kb + 1) * QB)
                d_probs = dot(vT[rows, kb * QB:(kb + 1) * QB], grad, 0, 0)
                p_s[h, tile, :] = (p_s[h, tile, :].astype(f32) * (d_probs - delta)).astype(bf16)
                yield

        def spread_back(qb):
            cols = slice(qb * QB, (qb + 1) * QB)
            depth, base = (qb + 1) * QB, strip_offset(qb)
            d_scores = p_s[h, base:base + depth, :]
            add_k = dot(qT[rows, cols], d_scores, 1, 1)
            if qb == NQ - 1:
                dacc_k[:, 0:depth] = add_k
            else:
                dacc_k[:, 0:depth] += add_k
            yield
            d_query = dot(kT[rows, 0:depth], d_scores, 1, 0) * HD ** -0.5
            side, lane = divmod(qb * QB, half)
            parts[0][pl.ds(pl.multiple_of(side * Dh + h * HD, HD), HD), lane:lane + QB] = unrotated(
                d_query.astype(bf16).astype(f32), cos_s[:, cols], sin_s[:, cols]
            ).astype(bf16)
            yield

        for _ in score_back(NQ - 1):
            pass
        for qb in reversed(range(NQ)):
            interleave(score_back(qb - 1) if qb else iter(()), qb + 1 if qb else 0, spread_back(qb), 2)
        for side in range(2):
            cols = slice(side * half, (side + 1) * half)
            place_rows = pl.ds(pl.multiple_of(side * Dh + h * HD, HD), HD)
            parts[1][place_rows, 0:half] = unrotated(
                dacc_k[:, cols].astype(bf16).astype(f32), cos_s[:, cols], sin_s[:, cols]
            ).astype(bf16)
            parts[2][place_rows, 0:half] = dacc_v[:, cols].astype(bf16)
        @pl.when(h == 0)
        def _():
            step_at("head 0")

        @pl.when(h == 1)
        def _():
            step_at("head 1")
            lin_grads(0)
            b1.begin()

        @pl.when(h == 2)
        def _():
            step_at("head 2")

    step_at("head 3")

    def back_norm(side, start):
        side_rows = pl.ds(pl.multiple_of(side * Dh, Dh), Dh)
        total = None
        for i in range(3):
            term = dot(parts[i][side_rows, pl.ds(start, MB)], wqkvT[i * Dh:(i + 1) * Dh, :], 0, 0)
            total = term if total is None else total + term
        return total

    @pl.loop(0, half // MB)
    def _(i):
        start = pl.multiple_of(i * MB, MB)
        nm[pl.ds(start, MB), :] = back_norm(1 - c, start).astype(bf16)

    dn_in = cots
    dn_copy = remote(nm, dn_in, dn_send.at[0], dn_recv.at[0], sib, z)
    dn_copy.start()
    step_at("parts")
    lin_grads(1)
    step_at("projections")
    back_wait(xs, (1 - c) * half, out, out_send, out_recv, loc_sem.at[pl.ds(2, per)])
    dn_copy.wait()

    g_ga[...] = jnp.zeros((8, D), f32)

    @pl.loop(0, NB)
    def _(i):
        start = pl.multiple_of(i * MB, MB)
        rows = pl.ds(start, MB)
        own = pl.ds(pl.multiple_of(c * half + start, MB), MB)
        d_normed = back_norm(c, start) + dn_in[rows, :].astype(f32)
        plain, inverse = rms(xs[own, :].astype(f32))
        scaled = d_normed * gain_a[...]
        g_ga[...] += fold_rows(d_normed * plain)
        d_start = inverse * (scaled - plain * jnp.mean(scaled * plain, axis=-1, keepdims=True))
        nm[rows, :] = (da[rows, :].astype(f32) + d_start).astype(bf16)

        @pl.when(i == 1)
        def _():
            step_at("gin 1")

        @pl.when(i == 2)
        def _():
            step_at("gin 2")

    step_at("gin 3")
    for k in range(D // quarter):
        features = slice(k * quarter, (k + 1) * quarter)
        gB[3 * D + 8 * k:3 * D + 8 * (k + 1), side_cols[1]] = g_ga[:, features].astype(bf16)
    b2.begin()
    for step in SCHEDULE["end"]:
        if step < 6:
            sums[step].advance()
        else:
            i = jnp.int32(step - 6)
            back_start(i, nm, i * MB, gin, gin_send, gin_recv, loc_sem.at[pl.ds(2 + per, per)])
    back_wait(nm, 0, gin, gin_send, gin_recv, loc_sem.at[pl.ds(2 + per, per)])


def on_device(
    G, S, NP,
    inputs, segment_ids, cotangent, norm_attn, norm_mlp, w_query, w_key, w_value, w_out, w_gate, w_up, w_down,
):
    _, T, D = inputs.shape
    FF = w_gate.shape[1]
    L = T * S
    half, Dh = L // 2, D // 2
    NH = Dh // HD
    anywhere = pl.BlockSpec(memory_space=pl.ANY)
    vmem = pl.BlockSpec(memory_space=pltpu.VMEM)
    dma = pltpu.SemaphoreType.DMA

    def buf(*shape, dtype=bf16):
        return pltpu.VMEM(shape, dtype)

    strips = strip_offset(L // QB)
    shards = NP * S
    RA, RB = padded(3 * FF + D + 16, shards), padded(3 * D + 32, shards)

    sizes = axis_sizes(NP, S)
    sum_scratch = []
    for k, (_, count) in enumerate(sum_rows(RA, RB, D, FF, shards)):
        over = [sizes[letter] for letter in AXES[k]]
        sum_scratch += [buf(*shape) for shape in lands(count, over, k < 4, Dh if k < 4 else Dh // 2)]
        sum_scratch += [dma((copies_of(over),)), dma((copies_of(over),))]
    NB, per = half // MB, T // MB
    out, gin, out_a, out_b = pl.pallas_call(
        functools.partial(block_kernel, G, S, NP, T, L, D, FF),
        out_shape=[
            jax.ShapeDtypeStruct((G, T, D), bf16),
            jax.ShapeDtypeStruct((G, T, D), bf16),
            jax.ShapeDtypeStruct((RA, D), bf16),
            jax.ShapeDtypeStruct((RB, D), bf16),
        ],
        in_specs=[anywhere, vmem, anywhere, vmem, vmem] + [anywhere] * 7,
        out_specs=[anywhere] * 4,
        scratch_shapes=[
            buf(L, D), buf(half, D), buf(G, L, dtype=jnp.int32), buf(8, L, dtype=f32),
            buf(HD // 2, L, dtype=f32), buf(HD // 2, L, dtype=f32),
            buf(L, D), buf(3 * Dh, D), buf(RA, D), buf(RB, D),
            buf(Dh, L), buf(Dh, L), buf(Dh, L),
            buf(NH, strips, QB), buf(2, L, QB, dtype=f32), buf(NH, 8, L, dtype=f32), buf(Dh, L), buf(D, half),
            buf(half, D), buf(half, FF), buf(half, FF), buf(half, FF),
            buf(half, D), buf(D, half),
            buf(Dh, L), buf(HD, L, dtype=f32), buf(HD, L, dtype=f32),
            buf(8, D, dtype=f32), buf(8, D, dtype=f32),
            dma((7,)), dma((2 + 2 * per,)), dma((2,)), dma((G,)), dma((S,)), dma((S,)), dma((G,)), dma((G,)),
            dma((NH,)), dma((NH,)), dma((NB,)), dma((G * per,)), dma((1,)), dma((1,)), dma((1,)), dma((1,)),
            dma((NB,)), dma((G * per,)), dma((6,)),
            *sum_scratch,
        ],
        compiler_params=pltpu.CompilerParams(
            collective_id=0, has_side_effects=True, vmem_limit_bytes=63 * 2**20
        ),
    )(
        inputs, segment_ids, cotangent, norm_attn.reshape(1, D), norm_mlp.reshape(1, D),
        w_query, w_key, w_value, w_out, w_gate.T, w_up.T, w_down,
    )

    moves = []
    for k in range(3):
        moves += [(1, k * FF + first, FF // 2, k, first) for first in (0, FF // 2)]
    moves.append((1, 3 * FF, D, 3, 0))
    moves += [(2, k * D, D, 4 + k, 0) for k in range(3)]
    moves += [(3, l * T, T, 7, l * T) for l in range(G)]

    def convert_kernel(out_ref, a_ref, b_ref, gin_ref, *rest):
        targets = rest[:8]
        final_out, gain_a_out, gain_m_out = rest[8:11]
        scratch = rest[11:]
        lows, wides = scratch[:len(moves)], scratch[len(moves):2 * len(moves)]
        tail_a, tail_b, out_low, read, write = scratch[2 * len(moves):]
        sources = (out_ref, a_ref, b_ref, gin_ref)
        last = len(moves)
        extra = [
            pltpu.make_async_copy(a_ref.at[pl.ds(3 * FF + D, 16)], tail_a, read.at[last]),
            pltpu.make_async_copy(b_ref.at[pl.ds(3 * D, 32)], tail_b, read.at[last + 1]),
            pltpu.make_async_copy(out_ref, out_low, read.at[last + 2]),
        ]
        reads, writes = [], []
        for k, (source, row, rows, target, to) in enumerate(moves):
            reads.append(pltpu.make_async_copy(sources[source].at[pl.ds(row, rows)], lows[k], read.at[k]))
            writes.append(pltpu.make_async_copy(wides[k], targets[target].at[pl.ds(to, rows)], write.at[k]))
        for copy in reads + extra:
            copy.start()
        for k in range(len(moves)):
            reads[k].wait()
            wides[k][...] = lows[k][...].astype(f32)
            writes[k].start()
        for copy in extra:
            copy.wait()
        final = pltpu.make_async_copy(out_low, final_out, write.at[last])
        final.start()
        gain_m_out[...] = jnp.sum(tail_a[0:8, :].astype(f32), axis=0)
        tail = tail_b[:, Dh // 2:Dh].astype(f32) + tail_b[:, Dh + Dh // 2:].astype(f32)
        gains = [jnp.sum(tail[8 * k:8 * (k + 1)], axis=0, keepdims=True) for k in range(4)]
        gain_a_out[...] = jnp.concatenate(gains, axis=1).reshape(D)
        for copy in writes + [final]:
            copy.wait()

    full = [(FF, D)] * 3 + [(D, D)] * 4 + [(G * T, D)]
    results = pl.pallas_call(
        convert_kernel,
        out_shape=[jax.ShapeDtypeStruct(shape, f32) for shape in full]
        + [jax.ShapeDtypeStruct((G * T, D), bf16), jax.ShapeDtypeStruct((D,), f32), jax.ShapeDtypeStruct((D,), f32)],
        in_specs=[anywhere] * 4,
        out_specs=[anywhere] * 9 + [vmem, vmem],
        scratch_shapes=[buf(move[2], D) for move in moves] + [buf(move[2], D, dtype=f32) for move in moves]
        + [buf(16, D), buf(32, D), buf(G * T, D), dma((len(moves) + 3,)), dma((len(moves) + 1,))],
        compiler_params=pltpu.CompilerParams(vmem_limit_bytes=62 * 2**20),
    )(out.reshape(G * T, D), out_a, out_b, gin.reshape(G * T, D))
    g_gate, g_up, g_down, g_out, g_query, g_key, g_value, grad_input, output, gain_attn, gain_mlp = results
    return (
        output.reshape(G, T, D), grad_input.reshape(G, T, D), gain_attn, gain_mlp,
        g_query, g_key, g_value, g_out, g_gate.T, g_up.T, g_down,
    )


def solution(mesh):
    S = mesh.shape["seq"]
    NP = mesh.shape["dp"] // 2
    rows = P("dp", "seq", None)
    return jax.shard_map(
        functools.partial(on_device, S // 2, S, NP),
        mesh=mesh,
        in_specs=(rows, P("dp", None), rows) + (P(),) * 9,
        out_specs=(rows, rows) + (P(),) * 9,
        check_vma=False,
    )
```
